32 devices in a mesh: section: 4 (over x, core), seq: 2 (over y), tp: 4 (over z).
Axes of the slice: x: 2, y: 2, z: 4, core: 2. Of those that a mesh axis runs over, the one named last changes fastest.
Arguments:
- streams: float32 [4, 4, 256, 1280], P('section', None, 'seq'), may hold values from -6 to 6
- head_streams: float32 [4, 256, 1280], P(None, 'seq'), may hold values from -6 to 6
- gains: float32 [4, 2, 1280], P('section'), may hold values from 0.1 to 1.9
- w_qkv: bfloat16 [4, 1280, 3, 1280], P('section', None, None, 'tp'), may hold values from -40 to 40
- w_out: bfloat16 [4, 1280, 1280], P('section', None, 'tp'), may hold values from -0.15625 to 0.15625
- w_up: bfloat16 [4, 1280, 5120], P('section', None, 'tp'), may hold values from -0.15625 to 0.15625
- w_down: bfloat16 [4, 1280, 5120], P('section', None, 'tp'), may hold values from -0.078125 to 0.078125
Outputs:
- recon: float32 [4, 4, 256, 1280], P('section', None, 'seq')
- grad_qkv: bfloat16 [4, 1280, 3, 1280], P('section', 'seq', None, 'tp')
- grad_out: bfloat16 [4, 1280, 1280], P('section', 'seq', 'tp')
- grad_up: bfloat16 [4, 1280, 5120], P('section', 'seq', 'tp')
- grad_down: bfloat16 [4, 1280, 5120], P('section', 'seq', 'tp')
The draws below stay inside these ranges and needn't reach their ends.
All inputs are finite; a program needn't handle non-finite values.
Results may differ from the reference program's by a relative error of at most 0.028.
Values may be sent and summed in bfloat16 or wider, within the bound.
No kernel may reach another device: no remote copies, remote signals or barrier semaphores. Data moves between devices by JAX's collectives and lax.ppermute only.
A program may use at most 128 MiB of HBM per device.

```python
import jax
import jax.numpy as jnp
from jax import lax

D = 1280
HEADS = 20
HEAD_DIM = 64
FF = 5120
TOK_DEV = 128
SECTIONS = 4
TOKENS = 256
N_SEQ = 2


def draw_w_qkv(key, part):
    scale = D ** (-0.5)
    base = jnp.clip(jax.random.normal(key, (SECTIONS, D, 3, D), jnp.float32), -6.0, 6.0)
    factor = jnp.where(jnp.arange(3) < 2, 1.4, 1.0)
    weight = base * scale * factor[None, None, :, None]
    return weight.astype(jnp.bfloat16)


def levels(rng, extent, shards, smallest, largest):
    def one(dim, blocks):
        steps = jax.random.uniform(jax.random.fold_in(jax.random.fold_in(rng, 6), dim), (blocks,), jnp.float32, smallest / len(shards), largest / len(shards))
        return jnp.repeat(jnp.exp(steps), extent[dim] // blocks).reshape((-1,) + (1,) * (len(extent) - dim - 1))

    loudness = one(*shards[0])
    for cut in shards[1:]:
        loudness = loudness * one(*cut)
    return loudness


def scatter_about(rng, extent, width, most, pieces=(), kind=jnp.bfloat16):
    drawn = jax.random.normal(rng, extent, jnp.float32) * width
    if len(pieces) > 0:
        drawn = levels(rng, extent, pieces, -0.22, 0.18) * drawn
    return jnp.clip(drawn, min=-most, max=most).astype(kind)


def setup_inputs(seed: int = 0) -> dict:
    seeds = jax.random.split(jax.random.key(seed), 8)
    return {
        "streams": scatter_about(seeds[0], (SECTIONS, 4, TOKENS, D), 1.0, 6.0, ((0, 4), (2, 2)), jnp.float32),
        "head_streams": scatter_about(seeds[1], (4, TOKENS, D), 1.0, 6.0, ((1, 2),), jnp.float32),
        "gains": jnp.clip(1.0 + 0.18 * jax.random.normal(seeds[2], (SECTIONS, 2, D), jnp.float32), 0.1, 1.9),
        "w_qkv": draw_w_qkv(jax.random.fold_in(seeds[7], 71), 0),
        "w_out": scatter_about(seeds[4], (SECTIONS, D, D), D ** -0.5, 0.15625, ((0, 4), (2, 4))),
        "w_up": scatter_about(seeds[5], (SECTIONS, D, FF), D ** -0.5, 0.15625, ((0, 4), (2, 4))),
        "w_down": scatter_about(seeds[6], (SECTIONS, D, FF), FF ** -0.5, 0.078125, ((0, 4), (2, 4))),
    }


def layer_norm(values, gain):
    centre = values - lax.optimization_barrier(jnp.mean(values, -1, keepdims=True))
    inv_std = lax.rsqrt(lax.optimization_barrier(jnp.mean(centre * centre, -1, keepdims=True)) + 1e-06)
    unit_vals = centre * inv_std
    return (unit_vals * gain, unit_vals, inv_std)

def norm_back(grad, gain, unit_vals, inv_std):
    scaled = grad * gain
    return inv_std * (scaled - lax.optimization_barrier(jnp.mean(scaled, -1, keepdims=True)) - unit_vals * lax.optimization_barrier(jnp.mean(scaled * unit_vals, -1, keepdims=True)))

def gelu_tanh(values):
    return jax.nn.gelu(values, approximate=True)

def attend_head(operands):
    query, keys, values, grad_mixed = operands
    scores = jnp.dot(query, keys.T, preferred_element_type=jnp.float32) * 0.125
    top = lax.optimization_barrier(jnp.max(scores, -1, keepdims=True))
    lse = top + jnp.log(lax.optimization_barrier(jnp.sum(jnp.exp(scores - top), -1, keepdims=True)))
    probs = jnp.exp(scores - lse)
    probs_low = probs.astype(jnp.bfloat16)
    mixed = jnp.dot(probs_low, values, preferred_element_type=jnp.float32).astype(jnp.bfloat16)
    grad_probs = jnp.dot(grad_mixed, values.T, preferred_element_type=jnp.float32)
    delta = lax.optimization_barrier(jnp.sum(probs * grad_probs, -1, keepdims=True))
    grad_scores = (probs * (grad_probs - delta)).astype(jnp.bfloat16)
    grad_query = (0.125 * jnp.dot(grad_scores, keys, preferred_element_type=jnp.float32)).astype(jnp.bfloat16)
    grad_keys = (0.125 * jnp.dot(grad_scores.T, query, preferred_element_type=jnp.float32)).astype(jnp.bfloat16)
    grad_values = jnp.dot(probs_low.T, grad_mixed, preferred_element_type=jnp.float32).astype(jnp.bfloat16)
    return (mixed, grad_query, grad_keys, grad_values)

def split_heads(values):
    return values.reshape(TOKENS, HEADS, HEAD_DIM).transpose(1, 0, 2)

def join_heads(values):
    return values.transpose(1, 0, 2).reshape(TOKENS, D)

def block(inputs, gain_pair, w_qkv, w_out, w_up, w_down):
    upper, lower, grad_upper, grad_lower = (inputs[0], inputs[1], inputs[2], inputs[3])
    normed_up, unit_up, inv_up = layer_norm(upper, gain_pair[1])
    normed_low = normed_up.astype(jnp.bfloat16)
    hidden_pre = jnp.dot(normed_low, w_up, preferred_element_type=jnp.float32)
    hidden = gelu_tanh(hidden_pre).astype(jnp.bfloat16)
    mlp_out = jnp.dot(hidden, w_down.T, preferred_element_type=jnp.float32)
    lower_in = lower - mlp_out
    normed_att, unit_att, inv_att = layer_norm(lower_in, gain_pair[0])
    att_low = normed_att.astype(jnp.bfloat16)
    w_flat = w_qkv.reshape(D, 3 * D)
    projected = jnp.dot(att_low, w_flat, preferred_element_type=jnp.float32).astype(jnp.bfloat16).reshape(TOKENS, 3, D)
    grad_lower_low = grad_lower.astype(jnp.bfloat16)
    grad_hidden = jnp.dot(grad_lower_low, w_down, preferred_element_type=jnp.float32)
    unused, pull = jax.vjp(gelu_tanh, hidden_pre)
    grad_pre = pull(grad_hidden)[0].astype(jnp.bfloat16)
    grad_normed = jnp.dot(grad_pre, w_up.T, preferred_element_type=jnp.float32)
    upper_total = grad_upper + norm_back(grad_normed, gain_pair[1], unit_up, inv_up)
    total_low = upper_total.astype(jnp.bfloat16)
    grad_mixed = jnp.dot(total_low, w_out, preferred_element_type=jnp.float32).astype(jnp.bfloat16)
    mixed, grad_query, grad_keys, grad_values = lax.map(attend_head, (split_heads(projected[:, 0]), split_heads(projected[:, 1]), split_heads(projected[:, 2]), split_heads(grad_mixed)))
    mixed = join_heads(mixed)
    att_out = jnp.dot(mixed, w_out.T, preferred_element_type=jnp.float32)
    upper_in = upper - att_out
    grad_proj = jnp.stack([join_heads(grad_query), join_heads(grad_keys), join_heads(grad_values)], 1).reshape(TOKENS, 3 * D)
    grad_att = jnp.dot(grad_proj, w_flat.T, preferred_element_type=jnp.float32)
    grad_lower_in = grad_lower + norm_back(grad_att, gain_pair[0], unit_att, inv_att)
    recon = jnp.stack([upper_in, lower_in, upper_total, grad_lower_in])
    factors = ((att_low, grad_proj), (total_low, mixed), (normed_low, grad_pre), (grad_lower_low, hidden))
    return (recon, factors)

def shard_terms(left, right):
    left_rows = left.astype(jnp.float32).reshape(N_SEQ, TOK_DEV, -1)
    right_rows = right.astype(jnp.float32).reshape(N_SEQ, TOK_DEV, -1)
    return jnp.einsum('ntd,nte->nde', left_rows, right_rows, precision=lax.Precision.HIGHEST)

def reference(streams, head_streams, gains, w_qkv, w_out, w_up, w_down):
    first = [block(streams[section], gains[section], w_qkv[section], w_out[section], w_up[section], w_down[section]) for section in range(SECTIONS)]
    recon_list = []
    grad_lists = [[], [], [], []]
    for section in range(SECTIONS):
        inputs = first[section + 1][0] if section + 1 < SECTIONS else head_streams
        recon, factors = block(inputs, gains[section], w_qkv[section], w_out[section], w_up[section], w_down[section])
        recon_list.append(recon)
        for index in range(4):
            totals = shard_terms(*first[section][1][index]) + shard_terms(*factors[index])
            part = lax.optimization_barrier(totals.astype(jnp.bfloat16))
            grad_lists[index].append(lax.optimization_barrier(jnp.sum(part.astype(jnp.float32), 0)).astype(jnp.bfloat16))
    grad_qkv = jnp.stack(grad_lists[0]).reshape(SECTIONS, D, 3, D)
    grad_out = jnp.stack(grad_lists[1])
    grad_up = jnp.stack(grad_lists[2])
    grad_down = jnp.stack(grad_lists[3])
    return (jnp.stack(recon_list), grad_qkv, grad_out, grad_up, grad_down)
```

```python
import jax
import jax.numpy as jnp
from jax import lax
from jax.sharding import PartitionSpec as P

HEAD_DIM = 64
BF16 = jnp.bfloat16
F32 = jnp.float32


def swap(shard, axis, by):
    length = lax.axis_size(axis)
    return lax.ppermute(shard, axis, [(i, i ^ by) for i in range(length)])


def shift(shard, axis, by):
    length = lax.axis_size(axis)
    return lax.ppermute(shard, axis, [(i, (i + by) % length) for i in range(length)])


def from_behind(shard, axis, by):
    length = lax.axis_size(axis)
    pairs = [(i, i + by) for i in range(length) if 0 <= i + by < length]
    return lax.ppermute(shard, axis, pairs)


def is_pow2(length):
    return length & (length - 1) == 0


def side(axis, by):
    return (lax.axis_index(axis) // by) % 2 == 1


def sum_rows(part, axis):
    length = lax.axis_size(axis)
    if not is_pow2(length):
        return lax.psum_scatter(part, axis, scatter_dimension=0, tiled=True)
    by = 1
    while by < length:
        half = part.shape[0] // 2
        upper = side(axis, by)
        low, high = part[:half], part[half:]
        got = swap(jnp.where(upper, low, high).astype(BF16), axis, by)
        part = jnp.where(upper, high, low).astype(F32) + got.astype(F32)
        by *= 2
    return part


def own_rows(whole, axis):
    length = lax.axis_size(axis)
    rows = whole.shape[0] // length
    index = lax.axis_index(axis)
    if is_pow2(length):
        place, by = 0, 1
        while by < length:
            place = place * 2 + (index // by) % 2
            by *= 2
    else:
        place = index
    return lax.dynamic_slice_in_dim(whole, place * rows, rows, 0)


def all_rows(shard, axis):
    length = lax.axis_size(axis)
    if not is_pow2(length):
        return lax.all_gather(shard, axis, axis=0, tiled=True)
    by = length // 2
    while by >= 1:
        got = swap(shard, axis, by)
        upper = side(axis, by)
        shard = jnp.concatenate([jnp.where(upper, got, shard), jnp.where(upper, shard, got)], 0)
        by //= 2
    return shard


def sum_all(part, axis):
    return all_rows(sum_rows(part, axis).astype(BF16), axis).astype(F32)


def layer_norm(values, gain):
    centre = values - jnp.mean(values, -1, keepdims=True)
    inv_std = lax.rsqrt(jnp.mean(centre * centre, -1, keepdims=True) + 1e-06)
    unit_vals = centre * inv_std
    return (unit_vals * gain, unit_vals, inv_std)


def norm_back(grad, gain, unit_vals, inv_std):
    scaled = grad * gain
    return inv_std * (
        scaled
        - jnp.mean(scaled, -1, keepdims=True)
        - unit_vals * jnp.mean(scaled * unit_vals, -1, keepdims=True)
    )


def gelu_tanh(values):
    return jax.nn.gelu(values, approximate=True)


def dot(left, right):
    return jnp.dot(left, right, preferred_element_type=F32)


def dot_t(left, right):
    return lax.dot_general(left, right, (((1,), (1,)), ((), ())), preferred_element_type=F32)


def t_dot(left, right):
    return lax.dot_general(left, right, (((0,), (0,)), ((), ())), preferred_element_type=F32)


def mlp_forward(upper, gain, w_up, w_down):
    normed, unit_up, inv_up = layer_norm(upper, gain)
    normed_low = normed.astype(BF16)
    pre = dot(normed_low, w_up)
    hidden = gelu_tanh(pre).astype(BF16)
    return normed_low, unit_up, inv_up, pre, hidden, dot_t(hidden, w_down)


def mlp_backward(grad_lower, pre, w_up, w_down):
    grad_lower_low = grad_lower.astype(BF16)
    grad_hidden = dot(grad_lower_low, w_down)
    pull = jax.vjp(gelu_tanh, pre)[1]
    grad_pre = pull(grad_hidden)[0].astype(BF16)
    return grad_lower_low, grad_pre, dot_t(grad_pre, w_up)


def to_heads(values):
    return values.reshape(values.shape[0], -1, HEAD_DIM)


def gather_seq(shard):
    length = lax.axis_size("seq")
    return jnp.concatenate([shard] + [shift(shard, "seq", -by) for by in range(1, length)], 0)


def attend(query, all_keys, all_values):
    scores = (
        jnp.einsum("qhd,khd->hqk", to_heads(query), to_heads(all_keys), preferred_element_type=F32)
        * 0.125
    )
    top = jnp.max(scores, -1, keepdims=True)
    lse = top + jnp.log(jnp.sum(jnp.exp(scores - top), -1, keepdims=True))
    probs = jnp.exp(scores - lse)
    mixed = jnp.einsum(
        "hqk,khd->qhd", probs.astype(BF16), to_heads(all_values), preferred_element_type=F32
    )
    return probs, mixed.astype(BF16).reshape(query.shape)


def attend_back(query, all_keys, all_values, probs, grad_mixed):
    rows = query.shape[0]
    grad_heads = to_heads(grad_mixed)
    grad_probs = jnp.einsum(
        "qhd,khd->hqk", grad_heads, to_heads(all_values), preferred_element_type=F32
    )
    delta = jnp.sum(probs * grad_probs, -1, keepdims=True)
    grad_scores = (probs * (grad_probs - delta)).astype(BF16)
    grad_query = 0.125 * jnp.einsum(
        "hqk,khd->qhd", grad_scores, to_heads(all_keys), preferred_element_type=F32
    )
    grad_keys = 0.125 * jnp.einsum(
        "hqk,qhd->khd", grad_scores, to_heads(query), preferred_element_type=F32
    )
    grad_values = jnp.einsum(
        "hqk,qhd->khd", probs.astype(BF16), grad_heads, preferred_element_type=F32
    )
    kv_grad = jnp.concatenate(
        [grad_keys.reshape(-1, query.shape[1]), grad_values.reshape(-1, query.shape[1])], 1
    )
    own = kv_grad[:rows]
    for by in range(1, lax.axis_size("seq")):
        other = kv_grad[by * rows : (by + 1) * rows].astype(BF16)
        own = own + shift(other, "seq", by).astype(F32)
    return jnp.concatenate([grad_query.astype(BF16).reshape(query.shape), own.astype(BF16)], 1)


def send_factors(pairs):
    length = lax.axis_size("seq")
    place = lax.axis_index("seq")
    width = pairs[0][0].shape[1] // length

    def cut(whole, index):
        return lax.dynamic_slice_in_dim(whole, index * width, width, 1)

    lefts = [[cut(left, place)] for left, unused in pairs]
    rights = [[right] for unused, right in pairs]
    for by in range(1, length):
        target = (place + by) % length
        packed = jnp.concatenate(
            [cut(left, target) for left, unused in pairs] + [right for unused, right in pairs], 1
        )
        got = shift(packed, "seq", by)
        at = 0
        for number in range(len(pairs)):
            lefts[number].append(got[:, at : at + width])
            at += width
        for number, (unused, right) in enumerate(pairs):
            rights[number].append(got[:, at : at + right.shape[1]])
            at += right.shape[1]
    return list(zip(lefts, rights))


def per_device(streams, head_streams, gains, w_qkv, w_out, w_up, w_down):
    gain_att, gain_mlp = gains[0, 0], gains[0, 1]
    width, local = w_qkv.shape[1], w_qkv.shape[3]
    w_flat = w_qkv[0].reshape(width, 3 * local)
    w_out, w_up, w_down = w_out[0], w_up[0], w_down[0]
    is_last = lax.axis_index("section") == lax.axis_size("section") - 1

    def back_a_block(shard):
        return from_behind(shard.astype(BF16), "section", -1)

    upper, lower, grad_upper, grad_lower = (streams[0, i] for i in range(4))
    mlp_terms, att_terms = [], []
    for tick in range(2):
        normed_low, unit_up, inv_up, pre, hidden, mlp_part = mlp_forward(
            upper, gain_mlp, w_up, w_down
        )
        mlp_out = sum_all(mlp_part, "tp")
        grad_lower_low, grad_pre, normed_part = mlp_backward(grad_lower, pre, w_up, w_down)
        grad_normed = sum_all(normed_part, "tp")
        mlp_terms.append(send_factors([(normed_low, grad_pre), (grad_lower_low, hidden)]))

        lower_in = lower - mlp_out
        normed_att, unit_att, inv_att = layer_norm(lower_in, gain_att)
        att_low = normed_att.astype(BF16)
        projected = dot(att_low, w_flat).astype(BF16)
        query = projected[:, :local]
        gathered = gather_seq(projected[:, local:])
        all_keys, all_values = gathered[:, :local], gathered[:, local:]
        probs, mixed = attend(query, all_keys, all_values)
        att_part = dot_t(mixed, w_out)

        upper_total = grad_upper + norm_back(grad_normed, gain_mlp, unit_up, inv_up)
        total_low = upper_total.astype(BF16)
        grad_mixed = dot(total_low, w_out).astype(BF16)
        grad_proj = attend_back(query, all_keys, all_values, probs, grad_mixed)
        att_grad_part = dot_t(grad_proj, w_flat)
        att_terms.append(send_factors([(att_low, grad_proj), (total_low, mixed)]))

        if tick == 0:
            next_lower = jnp.where(is_last, head_streams[1], back_a_block(lower_in).astype(F32))
            next_grad_upper = jnp.where(
                is_last, head_streams[2], back_a_block(upper_total).astype(F32)
            )
            upper_rows = own_rows(upper, "tp") - sum_rows(att_part, "tp")
            next_upper = all_rows(back_a_block(upper_rows), "tp").astype(F32)
            grad_rows = own_rows(grad_lower, "tp") + norm_back(
                sum_rows(att_grad_part, "tp"),
                gain_att,
                own_rows(unit_att, "tp"),
                own_rows(inv_att, "tp"),
            )
            next_grad_lower = all_rows(back_a_block(grad_rows), "tp").astype(F32)
            upper = jnp.where(is_last, head_streams[0], next_upper)
            grad_lower = jnp.where(is_last, head_streams[3], next_grad_lower)
            lower, grad_upper = next_lower, next_grad_upper

    upper_in = upper - sum_all(att_part, "tp")
    grad_att = sum_all(att_grad_part, "tp")
    grad_lower_in = grad_lower + norm_back(grad_att, gain_att, unit_att, inv_att)
    recon = jnp.stack([upper_in, lower_in, upper_total, grad_lower_in])[None]

    def weight_grad(terms, number):
        left = jnp.concatenate([part for tick in terms for part in tick[number][0]], 0)
        right = jnp.concatenate([part for tick in terms for part in tick[number][1]], 0)
        return t_dot(left, right).astype(BF16)

    return (
        recon,
        weight_grad(att_terms, 0).reshape(-1, 3, local)[None],
        weight_grad(att_terms, 1)[None],
        weight_grad(mlp_terms, 0)[None],
        weight_grad(mlp_terms, 1)[None],
    )


def solution(mesh):
    placed = (
        P("section", None, "seq", None),
        P(None, "seq", None),
        P("section", None, None),
        P("section", None, None, "tp"),
        P("section", None, "tp"),
        P("section", None, "tp"),
        P("section", None, "tp"),
    )
    return jax.shard_map(
        per_device,
        mesh=mesh,
        in_specs=placed,
        out_specs=(
            P("section", None, "seq", None),
            P("section", "seq", None, "tp"),
            P("section", "seq", "tp"),
            P("section", "seq", "tp"),
            P("section", "seq", "tp"),
        ),
        check_vma=False,
    )
```

```python
import functools

import jax
import jax.numpy as jnp
from jax import lax
from jax.experimental import pallas as pl
from jax.experimental.pallas import tpu as pltpu
from jax.sharding import PartitionSpec as P

HEAD_DIM = 64
BF16 = jnp.bfloat16
F32 = jnp.float32
LIMIT = 24 * 1024 * 1024
CHUNKS = 4
BLOCK = 256
GELU_SCALE = 0.7978845608028654
GELU_CUBE = 0.044715


def swap(shard, axis, by):
    length = lax.axis_size(axis)
    return lax.ppermute(shard, axis, [(i, i ^ by) for i in range(length)])


def shift(shard, axis, by):
    length = lax.axis_size(axis)
    return lax.ppermute(shard, axis, [(i, (i + by) % length) for i in range(length)])


def back_a_block(shard):
    length = lax.axis_size("section")
    return lax.ppermute(shard, "section", [(i, i - 1) for i in range(1, length)])


def back_to_pair(shard):
    length, pairs = lax.axis_size("section"), lax.axis_size("tp")
    crossed = [
        (i * pairs + j, (i - 1) * pairs + (j ^ 1)) for i in range(1, length) for j in range(pairs)
    ]
    return back_a_block(shard), lax.ppermute(shard, ("section", "tp"), crossed)


def call(body, outs, ins, scratch=(), token=None, aliases=(), after=()):
    spaces = {"vmem": pltpu.VMEM, "smem": pltpu.SMEM, "any": pl.ANY, "hbm": pl.ANY, "kept": pltpu.VMEM}
    ins, outs = list(ins), list(outs)
    n_ins, n_outs = len(ins), len(outs)
    ins += [(a, "any") for a in after]
    if token is not None:
        ins.append((token, "any"))
    outs.append(((8, 128), F32, "any"))

    def without_tokens(*refs):
        first = refs[:n_ins]
        rest = refs[len(ins) :]
        body(*first, *rest[:n_outs], *rest[n_outs + 1 :])

    arrays = [
        pltpu.with_memory_space_constraint(a, pltpu.HBM) if where == "hbm" else a for a, where in ins
    ]
    got = pl.pallas_call(
        without_tokens,
        out_shape=[
            (pltpu.VMEM if where == "kept" else jax.ShapeDtypeStruct)(shape, dtype)
            for shape, dtype, where in outs
        ],
        in_specs=[pl.BlockSpec(memory_space=spaces[where]) for unused, where in ins],
        out_specs=[pl.BlockSpec(memory_space=spaces[where]) for *unused, where in outs],
        scratch_shapes=list(scratch),
        input_output_aliases=dict(aliases),
        compiler_params=pltpu.CompilerParams(vmem_limit_bytes=LIMIT),
        cost_estimate=pl.CostEstimate(flops=1024, bytes_accessed=1024, transcendentals=0),
    )(*arrays)
    return got[:-1], got[-1]


def dot(left, right):
    return jnp.dot(left, right, preferred_element_type=F32)


def dot_t(left, right):
    return lax.dot_general(left, right, (((1,), (1,)), ((), ())), preferred_element_type=F32)


def t_dot(left, right):
    return lax.dot_general(left, right, (((0,), (0,)), ((), ())), preferred_element_type=F32)


def unit_norm(values):
    centre = values - jnp.mean(values, -1, keepdims=True)
    inv_std = lax.rsqrt(jnp.mean(centre * centre, -1, keepdims=True) + 1e-06)
    return centre * inv_std, inv_std


def norm_back(grad, gain, unit_vals, inv_std):
    scaled = grad * gain
    return inv_std * (
        scaled
        - jnp.mean(scaled, -1, keepdims=True)
        - unit_vals * jnp.mean(scaled * unit_vals, -1, keepdims=True)
    )


def rows_at(place, rows):
    return pl.ds(pl.multiple_of(place * rows, rows), rows)


def join(own_ref, got_ref, side, whole_ref):
    rows = own_ref.shape[0]
    whole_ref[rows_at(side, rows)] = own_ref[...].astype(F32)
    whole_ref[rows_at(1 - side, rows)] = got_ref[...].astype(F32)
    return whole_ref[...]


def split(whole_ref, side, send_ref, keep_ref):
    rows = send_ref.shape[0]
    send_ref[...] = whole_ref[rows_at(1 - side, rows)].astype(BF16)
    keep_ref[...] = whole_ref[rows_at(side, rows)]


def store_lefts(parts, keep_ref, message, place):
    width = parts[0].shape[1]
    if keep_ref is None:
        for number, part in enumerate(parts):
            message[:, number * width : (number + 1) * width] = part
        return 2 * width
    half = width // 2
    for number, part in enumerate(parts):
        at = slice(number * half, (number + 1) * half)

        @pl.when(place == 0)
        def first():
            keep_ref[:, at] = part[:, :half]
            message[:, at] = part[:, half:]

        @pl.when(place != 0)
        def second():
            keep_ref[:, at] = part[:, half:]
            message[:, at] = part[:, :half]

    return width


def start_all(copies):
    for copy in copies:
        copy.start()
    return copies


def row_chunks(whole, count):
    return [slice(i * whole // count, (i + 1) * whole // count) for i in range(count)]


def after_mlp_up(pre, hidden_ref, slope_ref, at):
    squared = pre * pre
    tanh = jnp.tanh(GELU_SCALE * pre * (1.0 + GELU_CUBE * squared))
    hidden_ref[:, at] = (0.5 * pre * (1.0 + tanh)).astype(BF16)
    slope_ref[:, at] = 0.5 * (1.0 + tanh) + 0.5 * pre * (1.0 - tanh * tanh) * (
        GELU_SCALE * (1.0 + 3.0 * GELU_CUBE * squared)
    )


def column_blocks(width, size):
    return [slice(at, min(at + size, width)) for at in range(0, width, size)]


def mlp_first_kernel(
    flags, gains, streams, w_up, w_down, normed_ref, hidden_ref, slope_ref, send, keep, unit_ref, inv_ref,
    upper, grad_lower, up_here, down_here, gains_here, sems, whole,
):
    up_cut, down_cut = row_chunks(up_here.shape[1], CHUNKS), row_chunks(down_here.shape[1], CHUNKS)
    firsts = start_all(
        [
            pltpu.make_async_copy(streams.at[0, 0], upper, sems.at[0]),
            pltpu.make_async_copy(gains, gains_here, sems.at[1]),
        ]
    )
    ups = start_all(
        [
            pltpu.make_async_copy(w_up.at[0, at], up_here.at[0, at], sems.at[3 + i])
            for i, at in enumerate(up_cut)
        ]
    )
    downs = start_all(
        [
            pltpu.make_async_copy(w_down.at[0, at], down_here.at[0, at], sems.at[3 + CHUNKS + i])
            for i, at in enumerate(down_cut)
        ]
    )
    last = pltpu.make_async_copy(streams.at[0, 3], grad_lower, sems.at[2])
    last.start()
    for copy in firsts:
        copy.wait()
    unit, inv_std = unit_norm(upper[...])
    normed_ref[...] = (unit * gains_here[1:2]).astype(BF16)
    unit_ref[...] = unit
    inv_ref[...] = jnp.broadcast_to(inv_std, inv_ref.shape)
    pre = None
    for i, at in enumerate(up_cut):
        ups[i].wait()
        part = dot(normed_ref[:, at], up_here[0, at])
        pre = part if pre is None else pre + part
    after_mlp_up(pre, hidden_ref, slope_ref, slice(None))
    for i, at in enumerate(down_cut):
        downs[i].wait()
        whole[:, at] = dot_t(hidden_ref[...], down_here[0, at])
    split(whole, flags[0], send, keep)
    last.wait()


def mlp_forward_kernel(
    flags, gains, own, got, head, w_up, w_down, normed_ref, hidden_ref, slope_ref, send, keep, unit_ref, inv_ref,
    upper_ref, whole,
):
    upper = jnp.where(flags[1] == 1, head[0], join(own, got, flags[0], whole))
    upper_ref[...] = upper
    unit, inv_std = unit_norm(upper)
    normed = (unit * gains[1:2]).astype(BF16)
    for at in column_blocks(hidden_ref.shape[1], BLOCK):
        after_mlp_up(dot(normed, w_up[0, :, at]), hidden_ref, slope_ref, at)
    whole[...] = dot_t(hidden_ref[...], w_down[0])
    split(whole, flags[0], send, keep)
    normed_ref[...] = normed
    unit_ref[...] = unit
    inv_ref[...] = jnp.broadcast_to(inv_std, inv_ref.shape)


def mlp_backward_kernel(later, flags, *refs):
    if later:
        own, got, head = refs[:3]
        refs = refs[3:]
    else:
        grad_lower_ref, refs = refs[0], refs[1:]
    slope, w_up, w_down, grad_pre_ref, send, keep = refs[:6]
    whole = refs[-1]
    if later:
        grad_lower_ref = refs[6]
        grad_lower = jnp.where(flags[1] == 1, head[3], join(own, got, flags[0], whole))
        grad_lower_ref[...] = grad_lower
    else:
        grad_lower = grad_lower_ref[...]
    grad_low = grad_lower.astype(BF16)
    for at in column_blocks(grad_pre_ref.shape[1], BLOCK):
        grad_pre_ref[:, at] = (dot(grad_low, w_down[0, :, at]) * slope[:, at]).astype(BF16)
    whole[...] = dot_t(grad_pre_ref[...], w_up[0])
    split(whole, flags[0], send, keep)


def pack_kernel(two, flags, first, second, *refs):
    if two:
        keep_left, message, rights = refs[-1], refs[-2], refs[:-2]
    else:
        keep_left, message, rights = None, refs[-1], refs[:-1]
    at = store_lefts([first[...], second[...].astype(BF16)], keep_left, message, flags[2])
    for ref in rights:
        message[:, at : at + ref.shape[1]] = ref[...]
        at += ref.shape[1]


def add_kernel(left, right, out):
    out[...] = (left[...].astype(F32) + right[...].astype(F32)).astype(BF16)


def add_pass_kernel(left, right, unused, out, unused_out):
    add_kernel(left, right, out)


def project_kernel(later, flags, gains, *refs):
    if later:
        before = refs[0]
        refs = refs[1:]
    source, own, got, w_qkv, lower_ref, att_low_ref, query_ref, kv_ref, unit_ref, inv_ref = refs[:10]
    lower_low, whole = refs[10:-1], refs[-1]
    if later:
        lower = jnp.where(flags[1] == 1, source[1], before[...].astype(F32))
    else:
        lower = source[0, 1]
    lower = lower - join(own, got, flags[0], whole)
    unit, inv_std = unit_norm(lower)
    att_low = (unit * gains[0:1]).astype(BF16)
    local = query_ref.shape[0]
    kv_ref[...] = dot_t(w_qkv[local:], att_low).astype(BF16)
    query_ref[...] = dot_t(w_qkv[:local], att_low).astype(BF16)
    lower_ref[...] = lower
    att_low_ref[...] = att_low
    unit_ref[...] = unit
    inv_ref[...] = jnp.broadcast_to(inv_std, inv_ref.shape)
    for ref in lower_low:
        ref[...] = lower.astype(BF16)


def attend_kernel(others, flags, *refs):
    query, kv = refs[0], refs[1 : 2 + others]
    w_out, probs_ref, mixed_ref, send, keep, whole = refs[2 + others :]
    local = query.shape[0]
    for head in range(local // HEAD_DIM):
        at = slice(head * HEAD_DIM, (head + 1) * HEAD_DIM)
        at_value = slice(local + head * HEAD_DIM, local + (head + 1) * HEAD_DIM)
        keys = jnp.concatenate([ref[at, :] for ref in kv], 1)
        values = jnp.concatenate([ref[at_value, :] for ref in kv], 1)
        scores = t_dot(keys, query[at, :]) * 0.125
        top = jnp.max(scores, 0, keepdims=True)
        weights = jnp.exp(scores - top)
        probs = weights * (1.0 / jnp.sum(weights, 0, keepdims=True))
        probs_ref[head] = probs
        mixed_ref[at, :] = dot(values, probs.astype(BF16)).astype(BF16)
    whole[...] = t_dot(mixed_ref[...], w_out[...])
    split(whole, flags[0], send, keep)


def attend_back_kernel(later, others, flags, gains, *refs):
    if later:
        before, refs = refs[0], refs[1:]
    source, unit, inv, own, got, query = refs[:6]
    kv = refs[6 : 7 + others]
    refs = refs[7 + others :]
    probs_ref, w_out, total_low_ref, grad_query, kv_own = refs[:5]
    kv_sent = refs[5 : 5 + others]
    totals, whole = refs[5 + others : -1], refs[-1]
    if later:
        total = jnp.where(flags[1] == 1, source[2], before[...].astype(F32))
    else:
        total = source[0, 2]
    grad_normed = join(own, got, flags[0], whole)
    total = total + norm_back(grad_normed, gains[1:2], unit[...], inv[:, 0:1])
    total_low = total.astype(BF16)
    grad_mixed = dot_t(w_out[...], total_low).astype(BF16)
    local, rows = query.shape
    for head in range(local // HEAD_DIM):
        at = slice(head * HEAD_DIM, (head + 1) * HEAD_DIM)
        at_value = slice(local + head * HEAD_DIM, local + (head + 1) * HEAD_DIM)
        keys = jnp.concatenate([ref[at, :] for ref in kv], 1)
        values = jnp.concatenate([ref[at_value, :] for ref in kv], 1)
        probs = probs_ref[head]
        grad_head = grad_mixed[at, :]
        grad_probs = t_dot(values, grad_head)
        delta = jnp.sum(probs * grad_probs, 0, keepdims=True)
        grad_scores = (probs * (grad_probs - delta)).astype(BF16)
        grad_query[at, :] = (0.125 * dot(keys, grad_scores)).astype(BF16)
        grad_keys = 0.125 * dot_t(query[at, :], grad_scores)
        grad_values = dot_t(grad_head, probs.astype(BF16))
        kv_own[at, :] = grad_keys[:, :rows]
        kv_own[at_value, :] = grad_values[:, :rows]
        for number, ref in enumerate(kv_sent):
            cols = slice((number + 1) * rows, (number + 2) * rows)
            ref[at, :] = grad_keys[:, cols].astype(BF16)
            ref[at_value, :] = grad_values[:, cols].astype(BF16)
    total_low_ref[...] = total_low
    for ref in totals:
        ref[...] = total


def project_back_kernel(others, passed, flags, *refs):
    grad_query, kv_own = refs[:2]
    kv_got = refs[2 : 2 + others]
    mixed, w_qkv = refs[2 + others : 4 + others]
    rights, send, keep = refs[4 + others + passed : 7 + others + passed]
    whole = refs[-1]
    local = mixed.shape[0]
    total = kv_own[...]
    for ref in kv_got:
        total = total + ref[...].astype(F32)
    rights[:local, :] = grad_query[...]
    rights[local : 3 * local, :] = total.astype(BF16)
    whole[...] = t_dot(rights[: 3 * local, :], w_qkv[...])
    split(whole, flags[0], send, keep)
    rights[3 * local :, :] = mixed[...]


def upper_boundary_kernel(flags, upper, own, got, out):
    total = (own[...].astype(F32) + got[...].astype(F32)).astype(BF16)
    out[...] = (upper[rows_at(flags[0], out.shape[0])] - total.astype(F32)).astype(BF16)


def lower_boundary_kernel(flags, gains, unit, inv, grad_lower, own, got, out):
    rows = rows_at(flags[0], out.shape[0])
    grad_att = (own[...].astype(F32) + got[...].astype(F32)).astype(BF16).astype(F32)
    back = norm_back(grad_att, gains[0:1], unit[rows], inv[rows][:, 0:1])
    out[...] = (grad_lower[rows] + back).astype(BF16)


def recon_middle_kernel(lower_in, total, out, sems):
    copies = start_all(
        [
            pltpu.make_async_copy(lower_in, out.at[0, 1], sems.at[0]),
            pltpu.make_async_copy(total, out.at[0, 2], sems.at[1]),
        ]
    )
    for copy in copies:
        copy.wait()


def recon_upper_kernel(flags, unused, upper, own, got, out, here, sem, whole):
    here[...] = upper[...] - join(own, got, flags[0], whole)
    copy = pltpu.make_async_copy(here, out.at[0, 0], sem)
    copy.start()
    copy.wait()


def recon_lower_kernel(flags, gains, unused, unit, inv, grad_lower, own, got, out, here, sem, whole):
    grad_att = join(own, got, flags[0], whole)
    here[...] = grad_lower[...] + norm_back(grad_att, gains[0:1], unit[...], inv[:, 0:1])
    copy = pltpu.make_async_copy(here, out.at[0, 3], sem)
    copy.start()
    copy.wait()


def mlp_grad_kernel(places, *refs):
    out = refs[-1]
    cut, width = out.shape
    left = jnp.concatenate([refs[i][:, at : at + cut] for i, at, unused, unused in places], 0)
    right = jnp.concatenate([refs[i][:, at : at + width] for unused, unused, i, at in places], 0)
    out[...] = t_dot(left, right).astype(BF16)


def att_grad_kernel(count, *refs):
    lefts, rights, qkv, out = refs[:count], refs[count : 2 * count], refs[2 * count], refs[2 * count + 1]
    cut, split_at = out.shape[1], qkv.shape[0]
    right = jnp.concatenate([ref[...] for ref in rights], 1)
    for number, (at, to) in enumerate([(slice(0, split_at), qkv), (slice(split_at, None), out)]):
        left = jnp.concatenate([ref[:, number * cut : (number + 1) * cut] for ref in lefts], 0)
        to[...] = dot(right[at], left).astype(BF16)


def send_message(keep, message, width):
    length = lax.axis_size("seq")
    if keep is not None:
        return [keep, shift(message, "seq", 1)]
    place = lax.axis_index("seq")
    cut = width // length

    def at(index):
        return jnp.concatenate(
            [
                lax.dynamic_slice_in_dim(message[:, :width], index * cut, cut, 1),
                lax.dynamic_slice_in_dim(message[:, width : 2 * width], index * cut, cut, 1),
                message[:, 2 * width :],
            ],
            1,
        )

    return [at(place)] + [
        shift(at((place + by) % length), "seq", by) for by in range(1, length)
    ]


def send_whole(part):
    return [part] + [shift(part, "seq", by) for by in range(1, lax.axis_size("seq"))]


def per_device(streams, head_streams, gains, w_qkv, w_out, w_up, w_down):
    width, local = w_qkv.shape[1], w_qkv.shape[3]
    rows = streams.shape[2]
    n_seq = lax.axis_size("seq")
    others = n_seq - 1
    hidden_width = w_up.shape[2]
    half = rows // 2
    gains = gains[0]
    w_qkv_t = jnp.transpose(w_qkv[0], (1, 2, 0)).reshape(3 * local, width)
    w_out_t = w_out[0].T
    is_last = lax.axis_index("section") == lax.axis_size("section") - 1
    flags = jnp.stack(
        [lax.axis_index("tp") % 2, is_last.astype(jnp.int32), lax.axis_index("seq")]
    ).astype(jnp.int32)
    flag, gain = (flags, "smem"), (gains, "vmem")
    whole, one_sem = pltpu.VMEM((rows, width), F32), pltpu.SemaphoreType.DMA
    full, low = ((rows, width), F32, "vmem"), ((rows, width), BF16, "vmem")
    halves = [((half, width), BF16, "vmem"), ((half, width), F32, "vmem")]
    half_low = halves[0]
    two = n_seq == 2

    def pack(first, second, *rights, **more):
        size = width * (1 if two else 2) + sum(right.shape[1] for right in rights)
        got = run(
            functools.partial(pack_kernel, two),
            [((rows, size), BF16, "vmem")] + [low] * two,
            [flag] + here(first, second, *rights),
            **more,
        )
        return (got[1] if two else None), got[0]

    hid_low = ((rows, hidden_width), BF16, "vmem")
    hid_full = ((rows, hidden_width), F32, "vmem")
    token = None

    def run(body, outs, ins, *rest, **more):
        nonlocal token
        got, token = call(body, outs, ins, *rest, token=token, **more)
        return got

    def here(*arrays):
        return [(a, "vmem") for a in arrays]

    def middle_adds(total):
        by = 2
        while by * 2 < lax.axis_size("tp"):
            (total,) = run(add_kernel, [half_low], here(total, swap(total, "tp", by)))
            by *= 2
        return total, (swap(total, "tp", by) if by < lax.axis_size("tp") else None)

    def add(left, right):
        if right is None:
            return left
        return run(add_kernel, [half_low], here(left, right))[0]

    def zero_if_none(got, like):
        return jnp.zeros_like(like) if got is None else got

    def add_pass(left, right, passed, **more):
        if right is None:
            return left, passed
        return run(
            add_pass_kernel,
            [half_low, (passed.shape, passed.dtype, "any")],
            here(left, right) + [(passed, "any")],
            aliases=[(2, 1)],
            **more,
        )

    norm_outs = [full, ((rows, 128), F32, "vmem")]
    cut = width // n_seq
    left_width = 2 * cut
    for tick in range(2):
        later = tick > 0
        mlp_outs = [low, hid_low, hid_full] + halves + norm_outs
        if later:
            normed, hidden, slope, send_f, keep_f, unit_up, inv_up, upper = run(
                mlp_forward_kernel,
                mlp_outs + [full],
                [flag, gain] + here(own_upper, got_upper, head_streams, up_here, down_here),
                [whole],
            )
            got_f = swap(send_f, "tp", 1)
            hidden_2 = send_whole(hidden)
            (next_grad,) = run(
                lower_boundary_kernel,
                [half_low],
                [flag, gain] + here(unit_att, inv_att, grad_lower, sum_b, zero_if_none(got_b, sum_b)),
            )
            own_grad, got_grad = back_to_pair(next_grad)
            sum_f, lower_low = add_pass(keep_f, got_f, lower_low)
            next_lower = back_a_block(lower_low)
            sum_f, got_f = middle_adds(sum_f)
            source = here(own_grad, got_grad, head_streams)
        else:
            got = run(
                mlp_first_kernel,
                mlp_outs + [full, full] + [(w.shape, BF16, "kept") for w in (w_up, w_down)],
                [flag] + [(a, "hbm") for a in (gains, streams, w_up, w_down)],
                [
                    pltpu.VMEM(gains.shape, F32),
                    pltpu.SemaphoreType.DMA((3 + 2 * CHUNKS,)),
                    whole,
                ],
            )
            normed, hidden, slope, send_f, keep_f, unit_up, inv_up, upper, grad_lower = got[:9]
            up_here, down_here = got[9:]
            got_f = swap(send_f, "tp", 1)
            hidden_1 = send_whole(hidden)
            source = here(grad_lower)
        got = run(
            functools.partial(mlp_backward_kernel, later),
            [hid_low] + halves + [full] * later,
            [flag] + source + here(slope, up_here, down_here),
            [whole],
        )
        grad_pre, send_b, keep_b = got[:3]
        if later:
            grad_lower = got[3]
        got_b = swap(send_b, "tp", 1)
        if later:
            own_out, total_low = add_pass(sum_f, got_f, total_low, after=rights_1[1:])
            got_out = swap(own_out, "tp", 1)
            next_total = back_a_block(total_low)
            factors_3 = send_message(*pack(normed, grad_lower), width)
            (sum_b,) = run(add_kernel, [half_low], here(keep_b, got_b))
            sum_b, got_b = middle_adds(sum_b)
        else:
            (sum_f,) = run(add_kernel, [half_low], here(keep_f, got_f))
            sum_f, got_f = middle_adds(sum_f)
            factors_0 = send_message(*pack(normed, grad_lower), width)
            own_out = add(sum_f, got_f)
            got_out = swap(own_out, "tp", 1)
            (sum_b,) = run(add_kernel, [half_low], here(keep_b, got_b), after=hidden_1[1:])
            sum_b, got_b = middle_adds(sum_b)
            grad_pre_1 = grad_pre

        source = here(next_lower, head_streams) if later else here(streams)
        got = run(
            functools.partial(project_kernel, later),
            [full, low, ((local, rows), BF16, "vmem"), ((2 * local, rows), BF16, "vmem")]
            + norm_outs
            + [low] * (not later),
            [flag, gain] + source + here(own_out, got_out, w_qkv_t),
            [whole],
            after=factors_1[1:] if later else factors_0[1:],
        )
        lower_in, att_low, query, kv, unit_att, inv_att = got[:6]
        if not later:
            lower_low = got[6]
        all_kv = [kv] + [shift(kv, "seq", -by) for by in range(1, n_seq)]
        own_normed = add(sum_b, got_b)
        got_normed = swap(own_normed, "tp", 1)
        probs, mixed, send_f, keep_f = run(
            functools.partial(attend_kernel, others),
            [((local // HEAD_DIM, n_seq * rows, rows), F32, "vmem"), ((local, rows), BF16, "vmem")]
            + halves,
            [flag] + here(query, *all_kv, w_out_t),
            [whole],
            after=hidden_2[1:] + factors_3[1:] if later else (),
        )
        got_f = swap(send_f, "tp", 1)

        got = run(
            functools.partial(attend_back_kernel, later, others),
            [low, ((local, rows), BF16, "vmem"), ((2 * local, rows), F32, "vmem")]
            + [((2 * local, rows), BF16, "vmem")] * others
            + [full] * later,
            [flag, gain]
            + (here(next_total, head_streams) if later else here(streams))
            + here(unit_up, inv_up, own_normed, got_normed, query, *all_kv, probs, w_out_t),
            [whole],
        )
        total_low, grad_query, kv_own = got[:3]
        kv_got = [shift(part, "seq", by + 1) for by, part in enumerate(got[3 : 3 + others])]
        (sum_f,) = run(add_kernel, [half_low], here(keep_f, got_f))
        sum_f, got_f = middle_adds(sum_f)
        if later:
            recon_out = [((1, 4, rows, width), F32, "any")]
            (recon,) = run(
                recon_middle_kernel, recon_out, here(lower_in, got[-1]), [pltpu.SemaphoreType.DMA((2,))]
            )
        got = run(
            functools.partial(project_back_kernel, others, int(later)),
            [((4 * local, rows), BF16, "vmem")] + halves + [(grad_pre.shape, BF16, "any")] * later,
            [flag] + here(grad_query, kv_own, *kv_got, mixed, w_qkv_t) + [(grad_pre, "any")] * later,
            [whole],
            aliases=[(5 + others, 3)] * later,
        )
        rights, send_b, keep_b = got[:3]
        got_b = swap(send_b, "tp", 1)
        rights_att = send_whole(rights)

        if later:
            rights_2 = rights_att
            grad_pre_2 = send_whole(got[3])
            factors_2 = send_message(*pack(att_low, total_low), width)
            own_f = add(sum_f, got_f)
            got_f = swap(own_f, "tp", 1)
            (sum_b,) = run(add_kernel, [half_low], here(keep_b, got_b))
            sum_b, got_b = middle_adds(sum_b)
        else:
            rights_1 = rights_att
            (next_half,) = run(
                upper_boundary_kernel,
                [half_low],
                [flag] + here(upper, sum_f, zero_if_none(got_f, sum_f)),
            )
            (sum_b,) = run(add_kernel, [half_low], here(keep_b, got_b))
            sum_b, got_b = middle_adds(sum_b)
            own_upper, got_upper = back_to_pair(next_half)
            factors_1 = send_message(*pack(att_low, total_low, grad_pre), width)

    ups = [(factors_0[0], 0, grad_pre_1, 0), (factors_3[0], 0, grad_pre_2[0], 0)]
    downs = [(factors_0[0], cut, hidden_1[0], 0), (factors_3[0], cut, hidden_2[0], 0)]
    for i in range(1, n_seq):
        ups += [(factors_0[i], 0, factors_1[i], left_width), (factors_3[i], 0, grad_pre_2[i], 0)]
        downs += [(factors_0[i], cut, hidden_1[i], 0), (factors_3[i], cut, hidden_2[i], 0)]

    def mlp_grad(terms):
        if not two:
            left = jnp.concatenate([a[:, at : at + cut] for a, at, unused, unused in terms], 0)
            right = jnp.concatenate([a[:, at : at + hidden_width] for unused, unused, a, at in terms], 0)
            return t_dot(left, right).astype(BF16)
        arrays, places = [], []
        for left, left_at, right, right_at in terms:
            for array in (left, right):
                if not any(array is known for known in arrays):
                    arrays.append(array)
            where = [next(i for i, known in enumerate(arrays) if known is a) for a in (left, right)]
            places.append((where[0], left_at, where[1], right_at))
        (grad,) = run(
            functools.partial(mlp_grad_kernel, places),
            [((cut, hidden_width), BF16, "vmem")],
            here(*arrays),
        )
        return grad

    grad_down = mlp_grad(downs)
    (recon,) = run(
        recon_upper_kernel,
        recon_out,
        [flag, (recon, "any")] + here(upper, own_f, got_f),
        [whole, one_sem, whole],
        aliases=[(1, 0)],
    )
    own_b = add(sum_b, got_b)
    got_b = swap(own_b, "tp", 1)
    grad_up = mlp_grad(ups)
    lefts_att, rights_att = factors_1 + factors_2, rights_1 + rights_2
    if two:
        grad_qkv, grad_out = run(
            functools.partial(att_grad_kernel, len(rights_att)),
            [((3 * local, cut), BF16, "vmem"), ((local, cut), BF16, "vmem")],
            here(*lefts_att, *rights_att),
        )
    else:
        right = jnp.concatenate(rights_att, 1)
        left = jnp.concatenate([a[:, :left_width] for a in lefts_att], 0)
        grad_qkv = dot(right[: 3 * local], left[:, :cut]).astype(BF16)
        grad_out = dot(right[3 * local :], left[:, cut:]).astype(BF16)
    (recon,) = run(
        recon_lower_kernel,
        recon_out,
        [flag, gain, (recon, "any")] + here(unit_att, inv_att, grad_lower, own_b, got_b),
        [whole, one_sem, whole],
        aliases=[(2, 0)],
    )
    return (
        recon,
        jnp.transpose(grad_qkv.reshape(3, local, cut), (2, 0, 1))[None],
        grad_out.T[None],
        grad_up[None],
        grad_down[None],
    )


def solution(mesh):
    placed = (
        P("section", None, "seq", None),
        P(None, "seq", None),
        P("section", None, None),
        P("section", None, None, "tp"),
        P("section", None, "tp"),
        P("section", None, "tp"),
        P("section", None, "tp"),
    )
    return jax.shard_map(
        per_device,
        mesh=mesh,
        in_specs=placed,
        out_specs=(
            P("section", None, "seq", None),
            P("section", "seq", None, "tp"),
            P("section", "seq", "tp"),
            P("section", "seq", "tp"),
            P("section", "seq", "tp"),
        ),
        check_vma=False,
    )
```

```python
import functools

import jax
import jax.numpy as jnp
from jax import lax
from jax.experimental import pallas as pl
from jax.experimental.pallas import tpu as pltpu
from jax.sharding import PartitionSpec as P

HEAD_DIM = 64
BF16 = jnp.bfloat16
F32 = jnp.float32
LIMIT = 24 * 1024 * 1024
CHUNKS = 4
BLOCK = 256
GELU_SCALE = 0.7978845608028654
GELU_CUBE = 0.044715


def swap(shard, axis, by):
    length = lax.axis_size(axis)
    return lax.ppermute(shard, axis, [(i, i ^ by) for i in range(length)])


def shift(shard, axis, by):
    length = lax.axis_size(axis)
    return lax.ppermute(shard, axis, [(i, (i + by) % length) for i in range(length)])


def back_a_block(shard):
    length = lax.axis_size("section")
    return lax.ppermute(shard, "section", [(i, i - 1) for i in range(1, length)])


def back_to_pair(shard):
    length, pairs = lax.axis_size("section"), lax.axis_size("tp")
    crossed = [
        (i * pairs + j, (i - 1) * pairs + (j ^ 1)) for i in range(1, length) for j in range(pairs)
    ]
    return back_a_block(shard), lax.ppermute(shard, ("section", "tp"), crossed)


def call(body, outs, ins, scratch=(), token=None, aliases=(), after=(), passed=()):
    spaces = {"vmem": pltpu.VMEM, "smem": pltpu.SMEM, "any": pl.ANY, "hbm": pl.ANY, "kept": pltpu.VMEM}
    ins, outs = list(ins), list(outs)
    n_ins, n_outs = len(ins), len(outs)
    aliases = list(aliases) + [(n_ins + i, n_outs + i) for i in range(len(passed))]
    ins += [(a, "any") for a in passed]
    outs += [(a.shape, a.dtype, "any") for a in passed]
    ins += [(a, "any") for a in after]
    if token is not None:
        ins.append((token, "any"))
    outs.append(((8, 128), F32, "any"))

    def without_tokens(*refs):
        first = refs[:n_ins]
        rest = refs[len(ins) :]
        body(*first, *rest[:n_outs], *rest[len(outs) :])

    arrays = [
        pltpu.with_memory_space_constraint(a, pltpu.HBM) if where == "hbm" else a for a, where in ins
    ]
    got = pl.pallas_call(
        without_tokens,
        out_shape=[
            (pltpu.VMEM if where == "kept" else jax.ShapeDtypeStruct)(shape, dtype)
            for shape, dtype, where in outs
        ],
        in_specs=[pl.BlockSpec(memory_space=spaces[where]) for unused, where in ins],
        out_specs=[pl.BlockSpec(memory_space=spaces[where]) for *unused, where in outs],
        scratch_shapes=list(scratch),
        input_output_aliases=dict(aliases),
        compiler_params=pltpu.CompilerParams(vmem_limit_bytes=LIMIT),
        cost_estimate=pl.CostEstimate(flops=1024, bytes_accessed=1024, transcendentals=0),
    )(*arrays)
    return got[:-1], got[-1]


def dot(left, right):
    return jnp.dot(left, right, preferred_element_type=F32)


def dot_t(left, right):
    return lax.dot_general(left, right, (((1,), (1,)), ((), ())), preferred_element_type=F32)


def t_dot(left, right):
    return lax.dot_general(left, right, (((0,), (0,)), ((), ())), preferred_element_type=F32)


def unit_norm(values):
    centre = values - jnp.mean(values, -1, keepdims=True)
    inv_std = lax.rsqrt(jnp.mean(centre * centre, -1, keepdims=True) + 1e-06)
    return centre * inv_std, inv_std


def norm_back(grad, gain, unit_vals, inv_std):
    scaled = grad * gain
    return inv_std * (
        scaled
        - jnp.mean(scaled, -1, keepdims=True)
        - unit_vals * jnp.mean(scaled * unit_vals, -1, keepdims=True)
    )


def rows_at(place, rows):
    return pl.ds(pl.multiple_of(place * rows, rows), rows)


def join(own_ref, got_ref, side, whole_ref):
    rows = own_ref.shape[0]
    whole_ref[rows_at(side, rows)] = own_ref[...].astype(F32)
    whole_ref[rows_at(1 - side, rows)] = got_ref[...].astype(F32)
    return whole_ref[...]


def split(whole_ref, side, send_ref, keep_ref):
    rows = send_ref.shape[0]
    send_ref[...] = whole_ref[rows_at(1 - side, rows)].astype(BF16)
    keep_ref[...] = whole_ref[rows_at(side, rows)]


def store_lefts(parts, keep_ref, message, place):
    width = parts[0].shape[1]
    if keep_ref is None:
        for number, part in enumerate(parts):
            message[:, number * width : (number + 1) * width] = part
        return len(parts) * width
    half = width // 2
    for number, part in enumerate(parts):
        at = slice(number * half, (number + 1) * half)

        @pl.when(place == 0)
        def first():
            keep_ref[:, at] = part[:, :half]
            message[:, at] = part[:, half:]

        @pl.when(place != 0)
        def second():
            keep_ref[:, at] = part[:, half:]
            message[:, at] = part[:, :half]

    return len(parts) * half


def start_all(copies):
    for number, copy in enumerate(copies):
        copy.start(priority=number % 2)
    return copies


def row_chunks(whole, count):
    return [slice(i * whole // count, (i + 1) * whole // count) for i in range(count)]


def after_mlp_up(pre, hidden_ref, slope_ref, at):
    squared = pre * pre
    tanh = jnp.tanh(GELU_SCALE * pre * (1.0 + GELU_CUBE * squared))
    hidden_ref[:, at] = (0.5 * pre * (1.0 + tanh)).astype(BF16)
    slope_ref[:, at] = 0.5 * (1.0 + tanh) + 0.5 * pre * (1.0 - tanh * tanh) * (
        GELU_SCALE * (1.0 + 3.0 * GELU_CUBE * squared)
    )


def column_blocks(width, size):
    return [slice(at, min(at + size, width)) for at in range(0, width, size)]


def after_left(message, hidden_width):
    return message.at[:, message.shape[1] - hidden_width :]


def mlp_first_kernel(
    flags, gains, streams, w_up, w_down, message, slope_ref, send, keep, unit_ref, inv_ref, upper, grad_lower,
    up_here, down_here, *refs,
):
    keep_left = refs[0] if len(refs) == 5 else None
    gains_here, normed_ref, sems, whole = refs[-4:]
    up_cut, down_cut = row_chunks(up_here.shape[1], CHUNKS), row_chunks(down_here.shape[1], CHUNKS)
    firsts = start_all(
        [
            pltpu.make_async_copy(streams.at[0, 0], upper, sems.at[0]),
            pltpu.make_async_copy(gains, gains_here, sems.at[1]),
        ]
    )
    ups = start_all(
        [
            pltpu.make_async_copy(w_up.at[0, at], up_here.at[0, at], sems.at[3 + i])
            for i, at in enumerate(up_cut)
        ]
    )
    downs = start_all(
        [
            pltpu.make_async_copy(w_down.at[0, at], down_here.at[0, at], sems.at[3 + CHUNKS + i])
            for i, at in enumerate(down_cut)
        ]
    )
    last = pltpu.make_async_copy(streams.at[0, 3], grad_lower, sems.at[2])
    last.start()
    for copy in firsts:
        copy.wait()
    unit, inv_std = unit_norm(upper[...])
    normed_ref[...] = (unit * gains_here[1:2]).astype(BF16)
    unit_ref[...] = unit
    inv_ref[...] = jnp.broadcast_to(inv_std, inv_ref.shape)
    store_lefts([normed_ref[...]], keep_left, message, flags[2])
    pre = None
    for i, at in enumerate(up_cut):
        ups[i].wait()
        part = dot(normed_ref[:, at], up_here[0, at])
        pre = part if pre is None else pre + part
    hidden = after_left(message, slope_ref.shape[1])
    after_mlp_up(pre, hidden, slope_ref, slice(None))
    for i, at in enumerate(down_cut):
        downs[i].wait()
        whole[:, at] = dot_t(hidden[...], down_here[0, at])
    split(whole, flags[0], send, keep)
    last.wait()


def mlp_forward_kernel(
    flags, gains, own, got, head, w_up, w_down, message, slope_ref, send, keep, unit_ref, inv_ref, upper_ref, *refs
):
    keep_left = refs[0] if len(refs) == 2 else None
    whole = refs[-1]
    upper = jnp.where(flags[1] == 1, head[0], join(own, got, flags[0], whole))
    upper_ref[...] = upper
    unit, inv_std = unit_norm(upper)
    normed = (unit * gains[1:2]).astype(BF16)
    hidden = after_left(message, slope_ref.shape[1])
    for at in column_blocks(slope_ref.shape[1], BLOCK):
        after_mlp_up(dot(normed, w_up[0, :, at]), hidden, slope_ref, at)
    whole[...] = dot_t(hidden[...], w_down[0])
    split(whole, flags[0], send, keep)
    unit_ref[...] = unit
    inv_ref[...] = jnp.broadcast_to(inv_std, inv_ref.shape)
    store_lefts([normed], keep_left, message, flags[2])


def mlp_backward_kernel(later, flags, *refs):
    if later:
        own, got, head = refs[:3]
        refs = refs[3:]
    else:
        grad_lower_ref, refs = refs[0], refs[1:]
    slope, w_up, w_down, message, send, keep = refs[:6]
    whole = refs[-1]
    refs = refs[6:-1]
    if later:
        grad_lower_ref, refs = refs[0], refs[1:]
        grad_lower = jnp.where(flags[1] == 1, head[3], join(own, got, flags[0], whole))
        grad_lower_ref[...] = grad_lower
    else:
        grad_lower = grad_lower_ref[...]
    grad_low = grad_lower.astype(BF16)
    grad_pre = after_left(message, slope.shape[1])
    for at in column_blocks(slope.shape[1], BLOCK):
        grad_pre[:, at] = (dot(grad_low, w_down[0, :, at]) * slope[:, at]).astype(BF16)
    whole[...] = dot_t(grad_pre[...], w_up[0])
    split(whole, flags[0], send, keep)
    store_lefts([grad_low], refs[0] if refs else None, message, flags[2])


def pack_kernel(two, flags, first, second, *refs):
    store_lefts([first[...], second[...]], refs[1] if two else None, refs[0], flags[2])


def add_kernel(left, right, out):
    out[...] = (left[...].astype(F32) + right[...].astype(F32)).astype(BF16)


def project_kernel(later, flags, gains, *refs):
    if later:
        before = refs[0]
        refs = refs[1:]
    source, own, got, w_qkv, lower_ref, att_low_ref, query_ref, kv_ref, unit_ref, inv_ref = refs[:10]
    lower_low, whole = refs[10:-1], refs[-1]
    if later:
        lower = jnp.where(flags[1] == 1, source[1], before[...].astype(F32))
    else:
        lower = source[0, 1]
    lower = lower - join(own, got, flags[0], whole)
    unit, inv_std = unit_norm(lower)
    att_low = (unit * gains[0:1]).astype(BF16)
    local = query_ref.shape[0]
    kv_ref[...] = dot_t(w_qkv[local:], att_low).astype(BF16)
    query_ref[...] = dot_t(w_qkv[:local], att_low).astype(BF16)
    lower_ref[...] = lower
    att_low_ref[...] = att_low
    unit_ref[...] = unit
    inv_ref[...] = jnp.broadcast_to(inv_std, inv_ref.shape)
    for ref in lower_low:
        ref[...] = lower.astype(BF16)


def attend_kernel(others, flags, *refs):
    query, kv = refs[0], refs[1 : 2 + others]
    w_out, probs_ref, mixed_ref, send, keep, whole = refs[2 + others :]
    local = query.shape[0]
    heads = [slice(at, at + HEAD_DIM) for at in range(0, local, HEAD_DIM)]
    keys = jnp.concatenate([ref[:local, :] for ref in kv], 1)
    values = jnp.concatenate([ref[local:, :] for ref in kv], 1)
    scores = [t_dot(keys[at], query[at, :]) * 0.125 for at in heads]
    weights = [jnp.exp(part - jnp.max(part, 0, keepdims=True)) for part in scores]
    probs = [part * (1.0 / jnp.sum(part, 0, keepdims=True)) for part in weights]
    mixed = [dot(values[at], part.astype(BF16)).astype(BF16) for at, part in zip(heads, probs)]
    for head, at in enumerate(heads):
        probs_ref[head] = probs[head]
        mixed_ref[at, :] = mixed[head]
    whole[...] = t_dot(mixed_ref[...], w_out[...])
    split(whole, flags[0], send, keep)


def attend_back_kernel(later, others, flags, gains, *refs):
    if later:
        before, refs = refs[0], refs[1:]
    source, unit, inv, own, got, query = refs[:6]
    kv = refs[6 : 7 + others]
    refs = refs[7 + others :]
    probs_ref, w_out, total_low_ref, grad_query, kv_own = refs[:5]
    kv_sent = refs[5 : 5 + others]
    totals, whole = refs[5 + others : -1], refs[-1]
    if later:
        total = jnp.where(flags[1] == 1, source[2], before[...].astype(F32))
    else:
        total = source[0, 2]
    grad_normed = join(own, got, flags[0], whole)
    total = total + norm_back(grad_normed, gains[1:2], unit[...], inv[:, 0:1])
    total_low = total.astype(BF16)
    grad_mixed = dot_t(w_out[...], total_low).astype(BF16)
    local, rows = query.shape
    heads = [slice(at, at + HEAD_DIM) for at in range(0, local, HEAD_DIM)]
    keys = jnp.concatenate([ref[:local, :] for ref in kv], 1)
    values = jnp.concatenate([ref[local:, :] for ref in kv], 1)
    probs = [probs_ref[head] for head in range(len(heads))]
    grad_probs = [t_dot(values[at], grad_mixed[at]) for at in heads]
    grad_scores = [
        (p * (g - jnp.sum(p * g, 0, keepdims=True))).astype(BF16) for p, g in zip(probs, grad_probs)
    ]
    grad_values = [dot_t(grad_mixed[at], p.astype(BF16)) for at, p in zip(heads, probs)]
    grad_keys = [0.125 * dot_t(query[at, :], g) for at, g in zip(heads, grad_scores)]
    for head, at in enumerate(heads):
        at_value = slice(local + at.start, local + at.stop)
        kv_own[at, :] = grad_keys[head][:, :rows]
        kv_own[at_value, :] = grad_values[head][:, :rows]
        for number, ref in enumerate(kv_sent):
            cols = slice((number + 1) * rows, (number + 2) * rows)
            ref[at, :] = grad_keys[head][:, cols].astype(BF16)
            ref[at_value, :] = grad_values[head][:, cols].astype(BF16)
        grad_query[at, :] = (0.125 * dot(keys[at], grad_scores[head])).astype(BF16)
    total_low_ref[...] = total_low
    for ref in totals:
        ref[...] = total


def project_back_kernel(others, flags, *refs):
    grad_query, kv_own = refs[:2]
    kv_got = refs[2 : 2 + others]
    mixed, w_qkv, rights, send, keep, whole = refs[2 + others :]
    local = mixed.shape[0]
    total = kv_own[...]
    for ref in kv_got:
        total = total + ref[...].astype(F32)
    rights[:local, :] = grad_query[...]
    rights[local : 3 * local, :] = total.astype(BF16)
    whole[...] = t_dot(rights[: 3 * local, :], w_qkv[...])
    split(whole, flags[0], send, keep)
    rights[3 * local :, :] = mixed[...]


def upper_boundary_kernel(flags, upper, own, got, out):
    total = (own[...].astype(F32) + got[...].astype(F32)).astype(BF16)
    out[...] = (upper[rows_at(flags[0], out.shape[0])] - total.astype(F32)).astype(BF16)


def lower_boundary_kernel(flags, gains, unit, inv, grad_lower, own, got, out):
    rows = rows_at(flags[0], out.shape[0])
    grad_att = (own[...].astype(F32) + got[...].astype(F32)).astype(BF16).astype(F32)
    back = norm_back(grad_att, gains[0:1], unit[rows], inv[rows][:, 0:1])
    out[...] = (grad_lower[rows] + back).astype(BF16)


def recon_middle_kernel(lower_in, total, out, sems):
    copies = start_all(
        [
            pltpu.make_async_copy(lower_in, out.at[0, 1], sems.at[0]),
            pltpu.make_async_copy(total, out.at[0, 2], sems.at[1]),
        ]
    )
    for copy in copies:
        copy.wait()


def recon_upper_kernel(flags, unused, upper, own, got, out, here, sem, whole):
    here[...] = upper[...] - join(own, got, flags[0], whole)
    copy = pltpu.make_async_copy(here, out.at[0, 0], sem)
    copy.start()
    copy.wait()


def recon_lower_kernel(flags, gains, unused, unit, inv, grad_lower, own, got, out, here, sem, whole):
    grad_att = join(own, got, flags[0], whole)
    here[...] = grad_lower[...] + norm_back(grad_att, gains[0:1], unit[...], inv[:, 0:1])
    copy = pltpu.make_async_copy(here, out.at[0, 3], sem)
    copy.start()
    copy.wait()


def mlp_grad_kernel(places, *refs):
    out = refs[-1]
    cut, width = out.shape
    left = jnp.concatenate([refs[i][:, at : at + cut] for i, at, unused, unused in places], 0)
    right = jnp.concatenate([refs[i][:, at : at + width] for unused, unused, i, at in places], 0)
    out[...] = t_dot(left, right).astype(BF16)


def att_grad_kernel(count, *refs):
    lefts, rights, qkv, out = refs[:count], refs[count : 2 * count], refs[2 * count], refs[2 * count + 1]
    cut, split_at = out.shape[1], qkv.shape[0]
    right = jnp.concatenate([ref[...] for ref in rights], 1)
    for number, (at, to) in enumerate([(slice(0, split_at), qkv), (slice(split_at, None), out)]):
        left = jnp.concatenate([ref[:, number * cut : (number + 1) * cut] for ref in lefts], 0)
        to[...] = dot(right[at], left).astype(BF16)


def send_message(keep, message, width, count):
    length = lax.axis_size("seq")
    if keep is not None:
        return [keep, shift(message, "seq", 1)]
    place = lax.axis_index("seq")
    cut = width // length

    def at(index):
        lefts = [
            lax.dynamic_slice_in_dim(message[:, i * width : (i + 1) * width], index * cut, cut, 1)
            for i in range(count)
        ]
        return jnp.concatenate(lefts + [message[:, count * width :]], 1)

    return [at(place)] + [
        shift(at((place + by) % length), "seq", by) for by in range(1, length)
    ]


def send_whole(part):
    return [part] + [shift(part, "seq", by) for by in range(1, lax.axis_size("seq"))]


def per_device(streams, head_streams, gains, w_qkv, w_out, w_up, w_down):
    width, local = w_qkv.shape[1], w_qkv.shape[3]
    rows = streams.shape[2]
    n_seq = lax.axis_size("seq")
    others = n_seq - 1
    hidden_width = w_up.shape[2]
    half = rows // 2
    gains = gains[0]
    w_qkv_t = jnp.transpose(w_qkv[0], (1, 2, 0)).reshape(3 * local, width)
    w_out_t = w_out[0].T
    is_last = lax.axis_index("section") == lax.axis_size("section") - 1
    flags = jnp.stack(
        [lax.axis_index("tp") % 2, is_last.astype(jnp.int32), lax.axis_index("seq")]
    ).astype(jnp.int32)
    flag, gain = (flags, "smem"), (gains, "vmem")
    whole, one_sem = pltpu.VMEM((rows, width), F32), pltpu.SemaphoreType.DMA
    full, low = ((rows, width), F32, "vmem"), ((rows, width), BF16, "vmem")
    halves = [((half, width), BF16, "vmem"), ((half, width), F32, "vmem")]
    half_low = halves[0]
    two = n_seq == 2

    left_size = width // 2 if two else width

    def pack(first, second, **more):
        got = run(
            functools.partial(pack_kernel, two),
            [((rows, 2 * left_size), BF16, "vmem")] + [low] * two,
            [flag] + here(first, second),
            **more,
        )
        return (got[1] if two else None), got[0]

    message_outs = [((rows, left_size + hidden_width), BF16, "vmem")]
    keep_outs = [((rows, left_size), BF16, "vmem")] * two
    hid_full = ((rows, hidden_width), F32, "vmem")
    token = None

    def run(body, outs, ins, *rest, **more):
        nonlocal token
        got, token = call(body, outs, ins, *rest, token=token, **more)
        return got

    def here(*arrays):
        return [(a, "vmem") for a in arrays]

    def middle_adds(total):
        by = 2
        while by * 2 < lax.axis_size("tp"):
            (total,) = run(add_kernel, [half_low], here(total, swap(total, "tp", by)))
            by *= 2
        return total, (swap(total, "tp", by) if by < lax.axis_size("tp") else None)

    def add(left, right, **more):
        if right is None:
            return left
        return run(add_kernel, [half_low], here(left, right), **more)[0]

    def zero_if_none(got, like):
        return jnp.zeros_like(like) if got is None else got

    norm_outs = [full, ((rows, 128), F32, "vmem")]
    cut = width // n_seq
    left_width = 2 * cut
    for tick in range(2):
        later = tick > 0
        mlp_outs = message_outs + [hid_full] + halves + norm_outs
        if later:
            got = run(
                mlp_forward_kernel,
                mlp_outs + [full] + keep_outs,
                [flag, gain] + here(own_upper, got_upper, head_streams, up_here, down_here),
                [whole],
            )
            message, slope, send_f, keep_f, unit_up, inv_up, upper = got[:7]
            got_f = swap(send_f, "tp", 1)
            message_2, factors_2 = message, send_message(got[7] if two else None, message, width, 1)
            (next_grad,) = run(
                lower_boundary_kernel,
                [half_low],
                [flag, gain] + here(unit_att, inv_att, grad_lower, sum_b, zero_if_none(got_b, sum_b)),
            )
            own_grad, got_grad = back_to_pair(next_grad)
            sum_f, lower_low, total_low = run(
                add_kernel, [half_low], here(keep_f, got_f), passed=[lower_low, total_low]
            )
            next_lower, next_total = back_a_block(lower_low), back_a_block(total_low)
            sum_f, got_f = middle_adds(sum_f)
            source = here(own_grad, got_grad, head_streams)
        else:
            got = run(
                mlp_first_kernel,
                mlp_outs + [full, full] + [(w.shape, BF16, "kept") for w in (w_up, w_down)] + keep_outs,
                [flag] + [(a, "hbm") for a in (gains, streams, w_up, w_down)],
                [
                    pltpu.VMEM(gains.shape, F32),
                    pltpu.VMEM((rows, width), BF16),
                    pltpu.SemaphoreType.DMA((3 + 2 * CHUNKS,)),
                    whole,
                ],
            )
            message, slope, send_f, keep_f, unit_up, inv_up, upper, grad_lower = got[:8]
            up_here, down_here = got[8:10]
            got_f = swap(send_f, "tp", 1)
            message_0, factors_0 = message, send_message(got[10] if two else None, message, width, 1)
            source = here(grad_lower)
        got = run(
            functools.partial(mlp_backward_kernel, later),
            message_outs + halves + [full] * later + keep_outs,
            [flag] + source + here(slope, up_here, down_here),
            [whole],
            after=rights_1[1:] + lefts_1[1:] if later else (),
        )
        message, send_b, keep_b = got[:3]
        keep_left = got[-1] if two else None
        if later:
            grad_lower = got[3]
        got_b = swap(send_b, "tp", 1)
        if later:
            message_3, factors_3 = message, send_message(keep_left, message, width, 1)
            own_out = add(sum_f, got_f)
            got_out = swap(own_out, "tp", 1)
            (sum_b,) = run(add_kernel, [half_low], here(keep_b, got_b))
            sum_b, got_b = middle_adds(sum_b)
        else:
            (sum_f,) = run(add_kernel, [half_low], here(keep_f, got_f))
            sum_f, got_f = middle_adds(sum_f)
            message_1, factors_1 = message, send_message(keep_left, message, width, 1)
            own_out = add(sum_f, got_f)
            got_out = swap(own_out, "tp", 1)
            (sum_b,) = run(add_kernel, [half_low], here(keep_b, got_b), after=())
            sum_b, got_b = middle_adds(sum_b)

        source = here(next_lower, head_streams) if later else here(streams)
        got = run(
            functools.partial(project_kernel, later),
            [full, low, ((local, rows), BF16, "vmem"), ((2 * local, rows), BF16, "vmem")]
            + norm_outs
            + [low] * (not later),
            [flag, gain] + source + here(own_out, got_out, w_qkv_t),
            [whole],
            after=() if later else factors_0[1:],
        )
        lower_in, att_low, query, kv, unit_att, inv_att = got[:6]
        if not later:
            lower_low = got[6]
        all_kv = [kv] + [shift(kv, "seq", -by) for by in range(1, n_seq)]
        own_normed = add(sum_b, got_b, after=() if later else ())
        got_normed = swap(own_normed, "tp", 1)
        probs, mixed, send_f, keep_f = run(
            functools.partial(attend_kernel, others),
            [((local // HEAD_DIM, n_seq * rows, rows), F32, "vmem"), ((local, rows), BF16, "vmem")]
            + halves,
            [flag] + here(query, *all_kv, w_out_t),
            [whole],
            after=factors_2[1:] if later else factors_1[1:],
        )
        got_f = swap(send_f, "tp", 1)

        got = run(
            functools.partial(attend_back_kernel, later, others),
            [low, ((local, rows), BF16, "vmem"), ((2 * local, rows), F32, "vmem")]
            + [((2 * local, rows), BF16, "vmem")] * others
            + [full] * later,
            [flag, gain]
            + (here(next_total, head_streams) if later else here(streams))
            + here(unit_up, inv_up, own_normed, got_normed, query, *all_kv, probs, w_out_t),
            [whole],
        )
        total_low, grad_query, kv_own = got[:3]
        kv_got = [shift(part, "seq", by + 1) for by, part in enumerate(got[3 : 3 + others])]
        (sum_f,) = run(add_kernel, [half_low], here(keep_f, got_f), after=factors_3[1:] if later else ())
        sum_f, got_f = middle_adds(sum_f)
        if later:
            recon_out = [((1, 4, rows, width), F32, "any")]
            (recon,) = run(
                recon_middle_kernel, recon_out, here(lower_in, got[-1]), [pltpu.SemaphoreType.DMA((2,))]
            )
        rights, send_b, keep_b = run(
            functools.partial(project_back_kernel, others),
            [((4 * local, rows), BF16, "vmem")] + halves,
            [flag] + here(grad_query, kv_own, *kv_got, mixed, w_qkv_t),
            [whole],
        )
        got_b = swap(send_b, "tp", 1)
        rights_att = send_whole(rights)

        if later:
            rights_2 = rights_att
            lefts_2 = send_message(*pack(att_low, total_low), width, 2)
            own_f = add(sum_f, got_f)
            got_f = swap(own_f, "tp", 1)
            (sum_b,) = run(add_kernel, [half_low], here(keep_b, got_b))
            sum_b, got_b = middle_adds(sum_b)
        else:
            rights_1 = rights_att
            (next_half,) = run(
                upper_boundary_kernel,
                [half_low],
                [flag] + here(upper, sum_f, zero_if_none(got_f, sum_f)),
            )
            (sum_b,) = run(add_kernel, [half_low], here(keep_b, got_b))
            sum_b, got_b = middle_adds(sum_b)
            own_upper, got_upper = back_to_pair(next_half)
            lefts_1 = send_message(*pack(att_low, total_low, after=[own_upper]), width, 2)

    ups, downs = [], []
    for up, down, mine_up, mine_down in (
        (factors_0, factors_1, message_1, message_0),
        (factors_2, factors_3, message_3, message_2),
    ):
        ups.append((up[0], 0, mine_up, left_size))
        downs.append((down[0], 0, mine_down, left_size))
        for i in range(1, n_seq):
            ups.append((up[i], 0, down[i], cut))
            downs.append((down[i], 0, up[i], cut))

    def mlp_grad(terms):
        if not two:
            left = jnp.concatenate([a[:, at : at + cut] for a, at, unused, unused in terms], 0)
            right = jnp.concatenate([a[:, at : at + hidden_width] for unused, unused, a, at in terms], 0)
            return t_dot(left, right).astype(BF16)
        arrays, places = [], []
        for left, left_at, right, right_at in terms:
            for array in (left, right):
                if not any(array is known for known in arrays):
                    arrays.append(array)
            where = [next(i for i, known in enumerate(arrays) if known is a) for a in (left, right)]
            places.append((where[0], left_at, where[1], right_at))
        (grad,) = run(
            functools.partial(mlp_grad_kernel, places),
            [((cut, hidden_width), BF16, "vmem")],
            here(*arrays),
        )
        return grad

    grad_down = mlp_grad(downs)
    (recon,) = run(
        recon_upper_kernel,
        recon_out,
        [flag, (recon, "any")] + here(upper, own_f, got_f),
        [whole, one_sem, whole],
        aliases=[(1, 0)],
    )
    grad_up = mlp_grad(ups)
    own_b = add(sum_b, got_b)
    got_b = swap(own_b, "tp", 1)
    lefts_att, rights_att = lefts_1 + lefts_2, rights_1 + rights_2
    if two:
        grad_qkv, grad_out = run(
            functools.partial(att_grad_kernel, len(rights_att)),
            [((3 * local, cut), BF16, "vmem"), ((local, cut), BF16, "vmem")],
            here(*lefts_att, *rights_att),
        )
    else:
        right = jnp.concatenate(rights_att, 1)
        left = jnp.concatenate([a[:, :left_width] for a in lefts_att], 0)
        grad_qkv = dot(right[: 3 * local], left[:, :cut]).astype(BF16)
        grad_out = dot(right[3 * local :], left[:, cut:]).astype(BF16)
    (recon,) = run(
        recon_lower_kernel,
        recon_out,
        [flag, gain, (recon, "any")] + here(unit_att, inv_att, grad_lower, own_b, got_b),
        [whole, one_sem, whole],
        aliases=[(2, 0)],
    )
    return (
        recon,
        jnp.transpose(grad_qkv.reshape(3, local, cut), (2, 0, 1))[None],
        grad_out.T[None],
        grad_up[None],
        grad_down[None],
    )


def solution(mesh):
    placed = (
        P("section", None, "seq", None),
        P(None, "seq", None),
        P("section", None, None),
        P("section", None, None, "tp"),
        P("section", None, "tp"),
        P("section", None, "tp"),
        P("section", None, "tp"),
    )
    return jax.shard_map(
        per_device,
        mesh=mesh,
        in_specs=placed,
        out_specs=(
            P("section", None, "seq", None),
            P("section", "seq", None, "tp"),
            P("section", "seq", "tp"),
            P("section", "seq", "tp"),
            P("section", "seq", "tp"),
        ),
        check_vma=False,
    )
```

```python
import functools

import jax
import jax.numpy as jnp
from jax import lax
from jax.experimental import pallas as pl
from jax.experimental.pallas import tpu as pltpu
from jax.sharding import PartitionSpec as P

HEAD_DIM = 64
BF16 = jnp.bfloat16
F32 = jnp.float32
LIMIT = 24 * 1024 * 1024
CHUNKS = 4
BLOCK = 256
GELU_SCALE = 0.7978845608028654
GELU_CUBE = 0.044715


def swap(shard, axis, by):
    length = lax.axis_size(axis)
    return lax.ppermute(shard, axis, [(i, i ^ by) for i in range(length)])


def shift(shard, axis, by):
    length = lax.axis_size(axis)
    return lax.ppermute(shard, axis, [(i, (i + by) % length) for i in range(length)])


def back_a_block(shard):
    length = lax.axis_size("section")
    return lax.ppermute(shard, "section", [(i, i - 1) for i in range(1, length)])


def back_to_pair(shard):
    length, pairs = lax.axis_size("section"), lax.axis_size("tp")
    crossed = [
        (i * pairs + j, (i - 1) * pairs + (j ^ 1)) for i in range(1, length) for j in range(pairs)
    ]
    other = lax.ppermute(shard, ("section", "tp"), crossed)
    return back_a_block(shard), other


def call(body, outs, ins, scratch=(), token=None, aliases=(), after=(), passed=()):
    spaces = {"vmem": pltpu.VMEM, "smem": pltpu.SMEM, "any": pl.ANY, "hbm": pl.ANY, "kept": pltpu.VMEM}
    ins, outs = list(ins), list(outs)
    n_ins, n_outs = len(ins), len(outs)
    aliases = list(aliases) + [(n_ins + i, n_outs + i) for i in range(len(passed))]
    ins += [(a, "any") for a in passed]
    outs += [(a.shape, a.dtype, "any") for a in passed]
    ins += [(a, "any") for a in after]
    if token is not None:
        ins.append((token, "any"))
    outs.append(((8, 128), F32, "any"))

    def without_tokens(*refs):
        first = refs[:n_ins]
        rest = refs[len(ins) :]
        body(*first, *rest[:n_outs], *rest[len(outs) :])

    arrays = [
        pltpu.with_memory_space_constraint(a, pltpu.HBM) if where == "hbm" else a for a, where in ins
    ]
    got = pl.pallas_call(
        without_tokens,
        out_shape=[
            (pltpu.VMEM if where == "kept" else jax.ShapeDtypeStruct)(shape, dtype)
            for shape, dtype, where in outs
        ],
        in_specs=[pl.BlockSpec(memory_space=spaces[where]) for unused, where in ins],
        out_specs=[pl.BlockSpec(memory_space=spaces[where]) for *unused, where in outs],
        scratch_shapes=list(scratch),
        input_output_aliases=dict(aliases),
        compiler_params=pltpu.CompilerParams(vmem_limit_bytes=LIMIT),
        cost_estimate=pl.CostEstimate(flops=1024, bytes_accessed=1024, transcendentals=0),
    )(*arrays)
    return got[:-1], got[-1]


def dot(left, right):
    return jnp.dot(left, right, preferred_element_type=F32)


def dot_t(left, right):
    return lax.dot_general(left, right, (((1,), (1,)), ((), ())), preferred_element_type=F32)


def t_dot(left, right):
    return lax.dot_general(left, right, (((0,), (0,)), ((), ())), preferred_element_type=F32)


def unit_norm(values):
    centre = values - jnp.mean(values, -1, keepdims=True)
    inv_std = lax.rsqrt(jnp.mean(centre * centre, -1, keepdims=True) + 1e-06)
    return centre * inv_std, inv_std


def norm_back(grad, gain, unit_vals, inv_std):
    scaled = grad * gain
    return inv_std * (
        scaled
        - jnp.mean(scaled, -1, keepdims=True)
        - unit_vals * jnp.mean(scaled * unit_vals, -1, keepdims=True)
    )


def rows_at(place, rows):
    return pl.ds(pl.multiple_of(place * rows, rows), rows)


def join(own_ref, got_ref, side, whole_ref):
    rows = own_ref.shape[0]
    whole_ref[rows_at(side, rows)] = own_ref[...].astype(F32)
    whole_ref[rows_at(1 - side, rows)] = got_ref[...].astype(F32)
    return whole_ref[...]


def split(whole_ref, side, send_ref, keep_ref):
    rows = send_ref.shape[0]
    send_ref[...] = whole_ref[rows_at(1 - side, rows)].astype(BF16)
    keep_ref[...] = whole_ref[rows_at(side, rows)]


def store_lefts(parts, keep_ref, message, place):
    width = parts[0].shape[1]
    if keep_ref is None:
        for number, part in enumerate(parts):
            message[:, number * width : (number + 1) * width] = part
        return len(parts) * width
    half = width // 2
    for number, part in enumerate(parts):
        at = slice(number * half, (number + 1) * half)

        @pl.when(place == 0)
        def first():
            keep_ref[:, at] = part[:, :half]
            message[:, at] = part[:, half:]

        @pl.when(place != 0)
        def second():
            keep_ref[:, at] = part[:, half:]
            message[:, at] = part[:, :half]

    return len(parts) * half


def start_all(copies):
    for copy in copies:
        copy.start()
    return copies


def row_chunks(whole, count):
    return [slice(i * whole // count, (i + 1) * whole // count) for i in range(count)]


def after_mlp_up(pre, hidden_ref, slope_ref, at):
    squared = pre * pre
    tanh = jnp.tanh(GELU_SCALE * pre * (1.0 + GELU_CUBE * squared))
    hidden_ref[:, at] = (0.5 * pre * (1.0 + tanh)).astype(BF16)
    slope_ref[:, at] = 0.5 * (1.0 + tanh) + 0.5 * pre * (1.0 - tanh * tanh) * (
        GELU_SCALE * (1.0 + 3.0 * GELU_CUBE * squared)
    )


def column_blocks(width, size):
    return [slice(at, min(at + size, width)) for at in range(0, width, size)]


def after_left(message, hidden_width):
    return message.at[:, message.shape[1] - hidden_width :]


def mlp_first_kernel(
    flags, gains, streams, w_up, message, slope_ref, unit_ref, inv_ref, upper, grad_lower, up_here, *refs
):
    keep_left = refs[0] if len(refs) == 4 else None
    gains_here, normed_ref, sems = refs[-3:]
    up_cut = row_chunks(up_here.shape[1], CHUNKS)
    firsts = start_all(
        [
            pltpu.make_async_copy(streams.at[0, 0], upper, sems.at[0]),
            pltpu.make_async_copy(gains, gains_here, sems.at[1]),
        ]
    )
    ups = start_all(
        [
            pltpu.make_async_copy(w_up.at[0, at], up_here.at[0, at], sems.at[3 + i])
            for i, at in enumerate(up_cut)
        ]
    )
    last = pltpu.make_async_copy(streams.at[0, 3], grad_lower, sems.at[2])
    last.start()
    for copy in firsts:
        copy.wait()
    unit, inv_std = unit_norm(upper[...])
    normed_ref[...] = (unit * gains_here[1:2]).astype(BF16)
    unit_ref[...] = unit
    inv_ref[...] = jnp.broadcast_to(inv_std, inv_ref.shape)
    pre = None
    for i, at in enumerate(up_cut):
        ups[i].wait()
        part = dot(normed_ref[:, at], up_here[0, at])
        pre = part if pre is None else pre + part
    after_mlp_up(pre, after_left(message, slope_ref.shape[1]), slope_ref, slice(None))
    store_lefts([normed_ref[...]], keep_left, message, flags[2])
    last.wait()


def mlp_first_down_kernel(flags, message, w_down, send, keep, whole):
    whole[...] = dot_t(after_left(message, w_down.shape[2])[...], w_down[0])
    split(whole, flags[0], send, keep)


def mlp_forward_kernel(
    flags, gains, own, got, head, w_up, w_down, message, slope_ref, send, keep, unit_ref, inv_ref, upper_ref, *refs
):
    keep_left = refs[0] if len(refs) == 2 else None
    whole = refs[-1]
    upper = jnp.where(flags[1] == 1, head[0], join(own, got, flags[0], whole))
    upper_ref[...] = upper
    unit, inv_std = unit_norm(upper)
    normed = (unit * gains[1:2]).astype(BF16)
    hidden = after_left(message, slope_ref.shape[1])
    for at in column_blocks(slope_ref.shape[1], BLOCK):
        after_mlp_up(dot(normed, w_up[0, :, at]), hidden, slope_ref, at)
    whole[...] = dot_t(hidden[...], w_down[0])
    split(whole, flags[0], send, keep)
    unit_ref[...] = unit
    inv_ref[...] = jnp.broadcast_to(inv_std, inv_ref.shape)
    store_lefts([normed], keep_left, message, flags[2])


def mlp_backward_kernel(later, flags, *refs):
    if later:
        own, got, head = refs[:3]
        refs = refs[3:]
    else:
        grad_lower_ref, refs = refs[0], refs[1:]
    slope, w_up, w_down, message, send, keep = refs[:6]
    whole = refs[-1]
    refs = refs[6:-1]
    if later:
        grad_lower_ref, refs = refs[0], refs[1:]
        grad_lower = jnp.where(flags[1] == 1, head[3], join(own, got, flags[0], whole))
        grad_lower_ref[...] = grad_lower
    else:
        grad_lower = grad_lower_ref[...]
    grad_low = grad_lower.astype(BF16)
    grad_pre = after_left(message, slope.shape[1])
    for at in column_blocks(slope.shape[1], BLOCK):
        grad_pre[:, at] = (dot(grad_low, w_down[0, :, at]) * slope[:, at]).astype(BF16)
    whole[...] = dot_t(grad_pre[...], w_up[0])
    split(whole, flags[0], send, keep)
    store_lefts([grad_low], refs[0] if refs else None, message, flags[2])


def pack_kernel(two, flags, first, second, *refs):
    store_lefts([first[...], second[...]], refs[1] if two else None, refs[0], flags[2])


def add_kernel(left, right, out):
    out[...] = (left[...].astype(F32) + right[...].astype(F32)).astype(BF16)


def project_kernel(later, flags, gains, *refs):
    if later:
        before = refs[0]
        refs = refs[1:]
    source, own, got, w_qkv, lower_ref, att_low_ref, query_ref, kv_ref, unit_ref, inv_ref = refs[:10]
    lower_low, whole = refs[10:-1], refs[-1]
    if later:
        lower = jnp.where(flags[1] == 1, source[1], before[...].astype(F32))
    else:
        lower = source[0, 1]
    lower = lower - join(own, got, flags[0], whole)
    unit, inv_std = unit_norm(lower)
    att_low = (unit * gains[0:1]).astype(BF16)
    local = query_ref.shape[0]
    kv_ref[...] = dot_t(w_qkv[local:], att_low).astype(BF16)
    query_ref[...] = dot_t(w_qkv[:local], att_low).astype(BF16)
    lower_ref[...] = lower
    att_low_ref[...] = att_low
    unit_ref[...] = unit
    inv_ref[...] = jnp.broadcast_to(inv_std, inv_ref.shape)
    for ref in lower_low:
        ref[...] = lower.astype(BF16)


def attend_kernel(others, flags, *refs):
    query, kv = refs[0], refs[1 : 2 + others]
    w_out, probs_ref, mixed_ref, send, keep, whole = refs[2 + others :]
    local = query.shape[0]
    heads = [slice(at, at + HEAD_DIM) for at in range(0, local, HEAD_DIM)]
    keys = jnp.concatenate([ref[:local, :] for ref in kv], 1)
    values = jnp.concatenate([ref[local:, :] for ref in kv], 1)
    scores = [t_dot(keys[at], query[at, :]) * 0.125 for at in heads]
    weights = [jnp.exp(part - jnp.max(part, 0, keepdims=True)) for part in scores]
    probs = [part * (1.0 / jnp.sum(part, 0, keepdims=True)) for part in weights]
    mixed = [dot(values[at], part.astype(BF16)).astype(BF16) for at, part in zip(heads, probs)]
    for head, at in enumerate(heads):
        probs_ref[head] = probs[head]
        mixed_ref[at, :] = mixed[head]
    whole[...] = t_dot(mixed_ref[...], w_out[...])
    split(whole, flags[0], send, keep)


def attend_back_kernel(later, others, flags, gains, *refs):
    if later:
        before, refs = refs[0], refs[1:]
    source, unit, inv, own, got, query = refs[:6]
    kv = refs[6 : 7 + others]
    refs = refs[7 + others :]
    probs_ref, w_out, total_low_ref, grad_query, kv_own = refs[:5]
    kv_sent = refs[5 : 5 + others]
    totals, whole = refs[5 + others : -1], refs[-1]
    if later:
        total = jnp.where(flags[1] == 1, source[2], before[...].astype(F32))
    else:
        total = source[0, 2]
    grad_normed = join(own, got, flags[0], whole)
    total = total + norm_back(grad_normed, gains[1:2], unit[...], inv[:, 0:1])
    total_low = total.astype(BF16)
    grad_mixed = dot_t(w_out[...], total_low).astype(BF16)
    local, rows = query.shape
    heads = [slice(at, at + HEAD_DIM) for at in range(0, local, HEAD_DIM)]
    keys = jnp.concatenate([ref[:local, :] for ref in kv], 1)
    values = jnp.concatenate([ref[local:, :] for ref in kv], 1)
    probs = [probs_ref[head] for head in range(len(heads))]
    grad_probs = [t_dot(values[at], grad_mixed[at]) for at in heads]
    grad_scores = [
        (p * (g - jnp.sum(p * g, 0, keepdims=True))).astype(BF16) for p, g in zip(probs, grad_probs)
    ]
    grad_values = [dot_t(grad_mixed[at], p.astype(BF16)) for at, p in zip(heads, probs)]
    grad_keys = [0.125 * dot_t(query[at, :], g) for at, g in zip(heads, grad_scores)]
    for head, at in enumerate(heads):
        at_value = slice(local + at.start, local + at.stop)
        kv_own[at, :] = grad_keys[head][:, :rows]
        kv_own[at_value, :] = grad_values[head][:, :rows]
        for number, ref in enumerate(kv_sent):
            cols = slice((number + 1) * rows, (number + 2) * rows)
            ref[at, :] = grad_keys[head][:, cols].astype(BF16)
            ref[at_value, :] = grad_values[head][:, cols].astype(BF16)
        grad_query[at, :] = (0.125 * dot(keys[at], grad_scores[head])).astype(BF16)
    total_low_ref[...] = total_low
    for ref in totals:
        ref[...] = total


def project_back_kernel(others, flags, *refs):
    grad_query, kv_own = refs[:2]
    kv_got = refs[2 : 2 + others]
    mixed, w_qkv, rights, send, keep, whole = refs[2 + others :]
    local = mixed.shape[0]
    total = kv_own[...]
    for ref in kv_got:
        total = total + ref[...].astype(F32)
    rights[:local, :] = grad_query[...]
    rights[local : 3 * local, :] = total.astype(BF16)
    whole[...] = t_dot(rights[: 3 * local, :], w_qkv[...])
    split(whole, flags[0], send, keep)
    rights[3 * local :, :] = mixed[...]


def upper_boundary_kernel(flags, upper, own, got, out):
    total = (own[...].astype(F32) + got[...].astype(F32)).astype(BF16)
    out[...] = (upper[rows_at(flags[0], out.shape[0])] - total.astype(F32)).astype(BF16)


def lower_boundary_kernel(flags, gains, unit, inv, grad_lower, own, got, out):
    rows = rows_at(flags[0], out.shape[0])
    grad_att = (own[...].astype(F32) + got[...].astype(F32)).astype(BF16).astype(F32)
    back = norm_back(grad_att, gains[0:1], unit[rows], inv[rows][:, 0:1])
    out[...] = (grad_lower[rows] + back).astype(BF16)


def recon_middle_kernel(lower_in, total, out, sems):
    copies = start_all(
        [
            pltpu.make_async_copy(lower_in, out.at[0, 1], sems.at[0]),
            pltpu.make_async_copy(total, out.at[0, 2], sems.at[1]),
        ]
    )
    for copy in copies:
        copy.wait()


def recon_upper_kernel(flags, unused, upper, own, got, out, here, sem, whole):
    here[...] = upper[...] - join(own, got, flags[0], whole)
    copy = pltpu.make_async_copy(here, out.at[0, 0], sem)
    copy.start()
    copy.wait()


def recon_lower_kernel(flags, gains, unused, unit, inv, grad_lower, own, got, out, here, sem, whole):
    grad_att = join(own, got, flags[0], whole)
    here[...] = grad_lower[...] + norm_back(grad_att, gains[0:1], unit[...], inv[:, 0:1])
    copy = pltpu.make_async_copy(here, out.at[0, 3], sem)
    copy.start()
    copy.wait()


def mlp_grad_kernel(places, *refs):
    out = refs[-1]
    cut, width = out.shape
    left = jnp.concatenate([refs[i][:, at : at + cut] for i, at, unused, unused in places], 0)
    right = jnp.concatenate([refs[i][:, at : at + width] for unused, unused, i, at in places], 0)
    out[...] = t_dot(left, right).astype(BF16)


def att_grad_kernel(count, *refs):
    lefts, rights, qkv, out = refs[:count], refs[count : 2 * count], refs[2 * count], refs[2 * count + 1]
    cut, split_at = out.shape[1], qkv.shape[0]
    right = jnp.concatenate([ref[...] for ref in rights], 1)
    for number, (at, to) in enumerate([(slice(0, split_at), qkv), (slice(split_at, None), out)]):
        left = jnp.concatenate([ref[:, number * cut : (number + 1) * cut] for ref in lefts], 0)
        to[...] = dot(right[at], left).astype(BF16)


def send_message(keep, message, width, count):
    length = lax.axis_size("seq")
    if keep is not None:
        return [keep, shift(message, "seq", 1)]
    place = lax.axis_index("seq")
    cut = width // length

    def at(index):
        lefts = [
            lax.dynamic_slice_in_dim(message[:, i * width : (i + 1) * width], index * cut, cut, 1)
            for i in range(count)
        ]
        return jnp.concatenate(lefts + [message[:, count * width :]], 1)

    return [at(place)] + [
        shift(at((place + by) % length), "seq", by) for by in range(1, length)
    ]


def send_whole(part):
    return [part] + [shift(part, "seq", by) for by in range(1, lax.axis_size("seq"))]


def per_device(streams, head_streams, gains, w_qkv, w_out, w_up, w_down):
    width, local = w_qkv.shape[1], w_qkv.shape[3]
    rows = streams.shape[2]
    n_seq = lax.axis_size("seq")
    others = n_seq - 1
    hidden_width = w_up.shape[2]
    half = rows // 2
    gains = gains[0]
    w_qkv_t = jnp.transpose(w_qkv[0], (1, 2, 0)).reshape(3 * local, width)
    w_out_t = w_out[0].T
    is_last = lax.axis_index("section") == lax.axis_size("section") - 1
    flags = jnp.stack(
        [lax.axis_index("tp") % 2, is_last.astype(jnp.int32), lax.axis_index("seq")]
    ).astype(jnp.int32)
    flag, gain = (flags, "smem"), (gains, "vmem")
    whole, one_sem = pltpu.VMEM((rows, width), F32), pltpu.SemaphoreType.DMA
    full, low = ((rows, width), F32, "vmem"), ((rows, width), BF16, "vmem")
    halves = [((half, width), BF16, "vmem"), ((half, width), F32, "vmem")]
    half_low = halves[0]
    two = n_seq == 2

    left_size = width // 2 if two else width

    def pack(first, second, **more):
        got = run(
            functools.partial(pack_kernel, two),
            [((rows, 2 * left_size), BF16, "vmem")] + [low] * two,
            [flag] + here(first, second),
            **more,
        )
        return (got[1] if two else None), got[0]

    message_outs = [((rows, left_size + hidden_width), BF16, "vmem")]
    keep_outs = [((rows, left_size), BF16, "vmem")] * two
    hid_full = ((rows, hidden_width), F32, "vmem")
    token = None

    def run(body, outs, ins, *rest, **more):
        nonlocal token
        got, token = call(body, outs, ins, *rest, token=token, **more)
        return got

    def here(*arrays):
        return [(a, "vmem") for a in arrays]

    def middle_adds(total):
        by = 2
        while by * 2 < lax.axis_size("tp"):
            (total,) = run(add_kernel, [half_low], here(total, swap(total, "tp", by)))
            by *= 2
        return total, (swap(total, "tp", by) if by < lax.axis_size("tp") else None)

    def add(left, right, **more):
        if right is None:
            return left
        return run(add_kernel, [half_low], here(left, right), **more)[0]

    def zero_if_none(got, like):
        return jnp.zeros_like(like) if got is None else got

    norm_outs = [full, ((rows, 128), F32, "vmem")]
    cut = width // n_seq
    left_width = 2 * cut
    for tick in range(2):
        later = tick > 0
        mlp_outs = message_outs + [hid_full] + halves + norm_outs
        if later:
            got = run(
                mlp_forward_kernel,
                mlp_outs + [full] + keep_outs,
                [flag, gain] + here(own_upper, got_upper, head_streams, up_here, w_down),
                [whole],
            )
            message, slope, send_f, keep_f, unit_up, inv_up, upper = got[:7]
            got_f = swap(send_f, "tp", 1)
            message_2, factors_2 = message, send_message(got[7] if two else None, message, width, 1)
            (next_grad,) = run(
                lower_boundary_kernel,
                [half_low],
                [flag, gain] + here(unit_att, inv_att, grad_lower, sum_b, zero_if_none(got_b, sum_b)),
            )
            own_grad, got_grad = back_to_pair(next_grad)
            sum_f, lower_low, total_low = run(
                add_kernel, [half_low], here(keep_f, got_f), passed=[lower_low, total_low]
            )
            next_lower, next_total = back_a_block(lower_low), back_a_block(total_low)
            sum_f, got_f = middle_adds(sum_f)
            source = here(own_grad, got_grad, head_streams)
        else:
            got = run(
                mlp_first_kernel,
                message_outs
                + [hid_full]
                + norm_outs
                + [full, full, (w_up.shape, BF16, "kept")]
                + keep_outs,
                [flag] + [(a, "hbm") for a in (gains, streams, w_up)],
                [
                    pltpu.VMEM(gains.shape, F32),
                    pltpu.VMEM((rows, width), BF16),
                    pltpu.SemaphoreType.DMA((3 + CHUNKS,)),
                ],
            )
            message, slope, unit_up, inv_up, upper, grad_lower, up_here = got[:7]
            send_f, keep_f = run(mlp_first_down_kernel, halves, [flag] + here(message, w_down), [whole])
            got_f = swap(send_f, "tp", 1)
            message_0, factors_0 = message, send_message(got[7] if two else None, message, width, 1)
            source = here(grad_lower)
        got = run(
            functools.partial(mlp_backward_kernel, later),
            message_outs + halves + [full] * later + keep_outs,
            [flag] + source + here(slope, up_here, w_down),
            [whole],
            after=rights_1[1:] + lefts_1[1:] if later else (),
        )
        message, send_b, keep_b = got[:3]
        keep_left = got[-1] if two else None
        if later:
            grad_lower = got[3]
        got_b = swap(send_b, "tp", 1)
        if later:
            message_3, factors_3 = message, send_message(keep_left, message, width, 1)
            own_out = add(sum_f, got_f)
            got_out = swap(own_out, "tp", 1)
            (sum_b,) = run(add_kernel, [half_low], here(keep_b, got_b))
            sum_b, got_b = middle_adds(sum_b)
        else:
            (sum_f,) = run(add_kernel, [half_low], here(keep_f, got_f))
            sum_f, got_f = middle_adds(sum_f)
            message_1, factors_1 = message, send_message(keep_left, message, width, 1)
            own_out = add(sum_f, got_f)
            got_out = swap(own_out, "tp", 1)
            (sum_b,) = run(add_kernel, [half_low], here(keep_b, got_b), after=())
            sum_b, got_b = middle_adds(sum_b)

        source = here(next_lower, head_streams) if later else here(streams)
        got = run(
            functools.partial(project_kernel, later),
            [full, low, ((local, rows), BF16, "vmem"), ((2 * local, rows), BF16, "vmem")]
            + norm_outs
            + [low] * (not later),
            [flag, gain] + source + here(own_out, got_out, w_qkv_t),
            [whole],
            after=() if later else factors_0[1:],
        )
        lower_in, att_low, query, kv, unit_att, inv_att = got[:6]
        if not later:
            lower_low = got[6]
        all_kv = [kv] + [shift(kv, "seq", -by) for by in range(1, n_seq)]
        own_normed = add(sum_b, got_b, after=() if later else ())
        got_normed = swap(own_normed, "tp", 1)
        probs, mixed, send_f, keep_f = run(
            functools.partial(attend_kernel, others),
            [((local // HEAD_DIM, n_seq * rows, rows), F32, "vmem"), ((local, rows), BF16, "vmem")]
            + halves,
            [flag] + here(query, *all_kv, w_out_t),
            [whole],
            after=factors_2[1:] if later else factors_1[1:],
        )
        got_f = swap(send_f, "tp", 1)

        got = run(
            functools.partial(attend_back_kernel, later, others),
            [low, ((local, rows), BF16, "vmem"), ((2 * local, rows), F32, "vmem")]
            + [((2 * local, rows), BF16, "vmem")] * others
            + [full] * later,
            [flag, gain]
            + (here(next_total, head_streams) if later else here(streams))
            + here(unit_up, inv_up, own_normed, got_normed, query, *all_kv, probs, w_out_t),
            [whole],
        )
        total_low, grad_query, kv_own = got[:3]
        kv_got = [shift(part, "seq", by + 1) for by, part in enumerate(got[3 : 3 + others])]
        (sum_f,) = run(add_kernel, [half_low], here(keep_f, got_f), after=factors_3[1:] if later else ())
        sum_f, got_f = middle_adds(sum_f)
        if later:
            recon_out = [((1, 4, rows, width), F32, "any")]
            (recon,) = run(
                recon_middle_kernel, recon_out, here(lower_in, got[-1]), [pltpu.SemaphoreType.DMA((2,))]
            )
        rights, send_b, keep_b = run(
            functools.partial(project_back_kernel, others),
            [((4 * local, rows), BF16, "vmem")] + halves,
            [flag] + here(grad_query, kv_own, *kv_got, mixed, w_qkv_t),
            [whole],
        )
        got_b = swap(send_b, "tp", 1)
        rights_att = send_whole(rights)

        if later:
            rights_2 = rights_att
            lefts_2 = send_message(*pack(att_low, total_low), width, 2)
            own_f = add(sum_f, got_f)
            got_f = swap(own_f, "tp", 1)
            (sum_b,) = run(add_kernel, [half_low], here(keep_b, got_b))
            sum_b, got_b = middle_adds(sum_b)
        else:
            rights_1 = rights_att
            (next_half,) = run(
                upper_boundary_kernel,
                [half_low],
                [flag] + here(upper, sum_f, zero_if_none(got_f, sum_f)),
            )
            (sum_b,) = run(add_kernel, [half_low], here(keep_b, got_b))
            sum_b, got_b = middle_adds(sum_b)
            own_upper, got_upper = back_to_pair(next_half)
            lefts_1 = send_message(*pack(att_low, total_low, after=[own_upper]), width, 2)

    ups, downs = [], []
    for up, down, mine_up, mine_down in (
        (factors_0, factors_1, message_1, message_0),
        (factors_2, factors_3, message_3, message_2),
    ):
        ups.append((up[0], 0, mine_up, left_size))
        downs.append((down[0], 0, mine_down, left_size))
        for i in range(1, n_seq):
            ups.append((up[i], 0, down[i], cut))
            downs.append((down[i], 0, up[i], cut))

    def mlp_grad(terms):
        if not two:
            left = jnp.concatenate([a[:, at : at + cut] for a, at, unused, unused in terms], 0)
            right = jnp.concatenate([a[:, at : at + hidden_width] for unused, unused, a, at in terms], 0)
            return t_dot(left, right).astype(BF16)
        arrays, places = [], []
        for left, left_at, right, right_at in terms:
            for array in (left, right):
                if not any(array is known for known in arrays):
                    arrays.append(array)
            where = [next(i for i, known in enumerate(arrays) if known is a) for a in (left, right)]
            places.append((where[0], left_at, where[1], right_at))
        (grad,) = run(
            functools.partial(mlp_grad_kernel, places),
            [((cut, hidden_width), BF16, "vmem")],
            here(*arrays),
        )
        return grad

    grad_down = mlp_grad(downs)
    (recon,) = run(
        recon_upper_kernel,
        recon_out,
        [flag, (recon, "any")] + here(upper, own_f, got_f),
        [whole, one_sem, whole],
        aliases=[(1, 0)],
    )
    grad_up = mlp_grad(ups)
    own_b = add(sum_b, got_b)
    got_b = swap(own_b, "tp", 1)
    lefts_att, rights_att = lefts_1 + lefts_2, rights_1 + rights_2
    if two:
        grad_qkv, grad_out = run(
            functools.partial(att_grad_kernel, len(rights_att)),
            [((3 * local, cut), BF16, "vmem"), ((local, cut), BF16, "vmem")],
            here(*lefts_att, *rights_att),
        )
    else:
        right = jnp.concatenate(rights_att, 1)
        left = jnp.concatenate([a[:, :left_width] for a in lefts_att], 0)
        grad_qkv = dot(right[: 3 * local], left[:, :cut]).astype(BF16)
        grad_out = dot(right[3 * local :], left[:, cut:]).astype(BF16)
    (recon,) = run(
        recon_lower_kernel,
        recon_out,
        [flag, gain, (recon, "any")] + here(unit_att, inv_att, grad_lower, own_b, got_b),
        [whole, one_sem, whole],
        aliases=[(2, 0)],
    )
    return (
        recon,
        jnp.transpose(grad_qkv.reshape(3, local, cut), (2, 0, 1))[None],
        grad_out.T[None],
        grad_up[None],
        grad_down[None],
    )


def solution(mesh):
    placed = (
        P("section", None, "seq", None),
        P(None, "seq", None),
        P("section", None, None),
        P("section", None, None, "tp"),
        P("section", None, "tp"),
        P("section", None, "tp"),
        P("section", None, "tp"),
    )
    return jax.shard_map(
        per_device,
        mesh=mesh,
        in_specs=placed,
        out_specs=(
            P("section", None, "seq", None),
            P("section", "seq", None, "tp"),
            P("section", "seq", "tp"),
            P("section", "seq", "tp"),
            P("section", "seq", "tp"),
        ),
        check_vma=False,
    )
```

```python
import functools

import jax
import jax.numpy as jnp
from jax import lax
from jax.experimental import pallas as pl
from jax.experimental.pallas import tpu as pltpu
from jax.sharding import PartitionSpec as P

HEAD_DIM = 64
BF16 = jnp.bfloat16
F32 = jnp.float32
LIMIT = 24 * 1024 * 1024
CHUNKS = 4
BLOCK = 256
GELU_SCALE = 0.7978845608028654
GELU_CUBE = 0.044715


def swap(shard, axis, by):
    length = lax.axis_size(axis)
    return lax.ppermute(shard, axis, [(i, i ^ by) for i in range(length)])


def shift(shard, axis, by):
    length = lax.axis_size(axis)
    return lax.ppermute(shard, axis, [(i, (i + by) % length) for i in range(length)])


def back_a_block(shard):
    length = lax.axis_size("section")
    return lax.ppermute(shard, "section", [(i, i - 1) for i in range(1, length)])


def back_to_pair(shard):
    length, pairs = lax.axis_size("section"), lax.axis_size("tp")
    crossed = [
        (i * pairs + j, (i - 1) * pairs + (j ^ 1)) for i in range(1, length) for j in range(pairs)
    ]
    other = lax.ppermute(shard, ("section", "tp"), crossed)
    return back_a_block(shard), other


def call(body, outs, ins, scratch=(), token=None, aliases=(), after=(), passed=()):
    spaces = {"vmem": pltpu.VMEM, "smem": pltpu.SMEM, "any": pl.ANY, "hbm": pl.ANY, "kept": pltpu.VMEM}
    ins, outs = list(ins), list(outs)
    n_ins, n_outs = len(ins), len(outs)
    aliases = list(aliases) + [(n_ins + i, n_outs + i) for i in range(len(passed))]
    ins += [(a, "any") for a in passed]
    outs += [(a.shape, a.dtype, "any") for a in passed]
    ins += [(a, "any") for a in after]
    if token is not None:
        ins.append((token, "any"))
    outs.append(((8, 128), F32, "any"))

    def without_tokens(*refs):
        first = refs[:n_ins]
        rest = refs[len(ins) :]
        body(*first, *rest[:n_outs], *rest[len(outs) :])

    arrays = [
        pltpu.with_memory_space_constraint(a, pltpu.HBM) if where == "hbm" else a for a, where in ins
    ]
    got = pl.pallas_call(
        without_tokens,
        out_shape=[
            (pltpu.VMEM if where == "kept" else jax.ShapeDtypeStruct)(shape, dtype)
            for shape, dtype, where in outs
        ],
        in_specs=[pl.BlockSpec(memory_space=spaces[where]) for unused, where in ins],
        out_specs=[pl.BlockSpec(memory_space=spaces[where]) for *unused, where in outs],
        scratch_shapes=list(scratch),
        input_output_aliases=dict(aliases),
        compiler_params=pltpu.CompilerParams(vmem_limit_bytes=LIMIT),
        cost_estimate=pl.CostEstimate(flops=1024, bytes_accessed=1024, transcendentals=0),
    )(*arrays)
    return got[:-1], got[-1]


def dot(left, right):
    return jnp.dot(left, right, preferred_element_type=F32)


def dot_t(left, right):
    return lax.dot_general(left, right, (((1,), (1,)), ((), ())), preferred_element_type=F32)


def t_dot(left, right):
    return lax.dot_general(left, right, (((0,), (0,)), ((), ())), preferred_element_type=F32)


def unit_norm(values):
    centre = values - jnp.mean(values, -1, keepdims=True)
    inv_std = lax.rsqrt(jnp.mean(centre * centre, -1, keepdims=True) + 1e-06)
    return centre * inv_std, inv_std


def norm_back(grad, gain, unit_vals, inv_std):
    scaled = grad * gain
    return inv_std * (
        scaled
        - jnp.mean(scaled, -1, keepdims=True)
        - unit_vals * jnp.mean(scaled * unit_vals, -1, keepdims=True)
    )


def rows_at(place, rows):
    return pl.ds(pl.multiple_of(place * rows, rows), rows)


def join(own_ref, got_ref, side, whole_ref):
    rows = own_ref.shape[0]
    whole_ref[rows_at(side, rows)] = own_ref[...].astype(F32)
    whole_ref[rows_at(1 - side, rows)] = got_ref[...].astype(F32)
    return whole_ref[...]


def split(whole_ref, side, send_ref, keep_ref):
    rows = send_ref.shape[0]
    send_ref[...] = whole_ref[rows_at(1 - side, rows)].astype(BF16)
    keep_ref[...] = whole_ref[rows_at(side, rows)]


def store_lefts(parts, keep_ref, message, place):
    width = parts[0].shape[1]
    if keep_ref is None:
        for number, part in enumerate(parts):
            message[:, number * width : (number + 1) * width] = part
        return len(parts) * width
    half = width // 2
    for number, part in enumerate(parts):
        at = slice(number * half, (number + 1) * half)

        @pl.when(place == 0)
        def first():
            keep_ref[:, at] = part[:, :half]
            message[:, at] = part[:, half:]

        @pl.when(place != 0)
        def second():
            keep_ref[:, at] = part[:, half:]
            message[:, at] = part[:, :half]

    return len(parts) * half


def start_all(copies):
    for copy in copies:
        copy.start()
    return copies


def row_chunks(whole, count):
    return [slice(i * whole // count, (i + 1) * whole // count) for i in range(count)]


def after_mlp_up(pre, hidden_ref, slope_ref, at):
    squared = pre * pre
    tanh = jnp.tanh(GELU_SCALE * pre * (1.0 + GELU_CUBE * squared))
    hidden_ref[:, at] = (0.5 * pre * (1.0 + tanh)).astype(BF16)
    slope_ref[:, at] = 0.5 * (1.0 + tanh) + 0.5 * pre * (1.0 - tanh * tanh) * (
        GELU_SCALE * (1.0 + 3.0 * GELU_CUBE * squared)
    )


def column_blocks(width, size):
    return [slice(at, min(at + size, width)) for at in range(0, width, size)]


def after_left(message, hidden_width):
    return message.at[:, message.shape[1] - hidden_width :]


def mlp_first_kernel(
    flags, gains, streams, w_up, message, slope_ref, unit_ref, inv_ref, upper, grad_lower, up_here, *refs
):
    keep_left = refs[0] if len(refs) == 4 else None
    gains_here, normed_ref, sems = refs[-3:]
    up_cut = row_chunks(up_here.shape[1], CHUNKS)
    firsts = start_all(
        [
            pltpu.make_async_copy(streams.at[0, 0], upper, sems.at[0]),
            pltpu.make_async_copy(gains, gains_here, sems.at[1]),
        ]
    )
    ups = start_all(
        [
            pltpu.make_async_copy(w_up.at[0, at], up_here.at[0, at], sems.at[3 + i])
            for i, at in enumerate(up_cut)
        ]
    )
    last = pltpu.make_async_copy(streams.at[0, 3], grad_lower, sems.at[2])
    last.start()
    for copy in firsts:
        copy.wait()
    unit, inv_std = unit_norm(upper[...])
    normed_ref[...] = (unit * gains_here[1:2]).astype(BF16)
    unit_ref[...] = unit
    inv_ref[...] = jnp.broadcast_to(inv_std, inv_ref.shape)
    pre = None
    for i, at in enumerate(up_cut):
        ups[i].wait()
        part = dot(normed_ref[:, at], up_here[0, at])
        pre = part if pre is None else pre + part
    after_mlp_up(pre, after_left(message, slope_ref.shape[1]), slope_ref, slice(None))
    store_lefts([normed_ref[...]], keep_left, message, flags[2])
    last.wait()


def mlp_first_down_kernel(flags, message, w_down, send, keep, whole):
    whole[...] = dot_t(after_left(message, w_down.shape[2])[...], w_down[0])
    split(whole, flags[0], send, keep)


def mlp_forward_kernel(
    flags, gains, got, own, head, w_up, w_down, message, slope_ref, send, keep, unit_ref, inv_ref, upper_ref, *refs
):
    keep_left = refs[0] if len(refs) == 2 else None
    whole = refs[-1]
    upper = jnp.where(flags[1] == 1, head[0], join(own, got, flags[0], whole))
    upper_ref[...] = upper
    unit, inv_std = unit_norm(upper)
    normed = (unit * gains[1:2]).astype(BF16)
    hidden = after_left(message, slope_ref.shape[1])
    for at in column_blocks(slope_ref.shape[1], BLOCK):
        after_mlp_up(dot(normed, w_up[0, :, at]), hidden, slope_ref, at)
    whole[...] = dot_t(hidden[...], w_down[0])
    split(whole, flags[0], send, keep)
    unit_ref[...] = unit
    inv_ref[...] = jnp.broadcast_to(inv_std, inv_ref.shape)
    store_lefts([normed], keep_left, message, flags[2])


def mlp_backward_kernel(later, flags, *refs):
    if later:
        own, got, head = refs[:3]
        refs = refs[3:]
    else:
        grad_lower_ref, refs = refs[0], refs[1:]
    slope, w_up, w_down, message, send, keep = refs[:6]
    whole = refs[-1]
    refs = refs[6:-1]
    if later:
        grad_lower_ref, refs = refs[0], refs[1:]
        grad_lower = jnp.where(flags[1] == 1, head[3], join(own, got, flags[0], whole))
        grad_lower_ref[...] = grad_lower
    else:
        grad_lower = grad_lower_ref[...]
    grad_low = grad_lower.astype(BF16)
    grad_pre = after_left(message, slope.shape[1])
    for at in column_blocks(slope.shape[1], BLOCK):
        grad_pre[:, at] = (dot(grad_low, w_down[0, :, at]) * slope[:, at]).astype(BF16)
    whole[...] = dot_t(grad_pre[...], w_up[0])
    split(whole, flags[0], send, keep)
    store_lefts([grad_low], refs[0] if refs else None, message, flags[2])


def pack_kernel(two, flags, first, second, *refs):
    store_lefts([first[...], second[...]], refs[1] if two else None, refs[0], flags[2])


def add_kernel(left, right, out):
    out[...] = (left[...].astype(F32) + right[...].astype(F32)).astype(BF16)


def project_kernel(later, flags, gains, *refs):
    if later:
        before = refs[0]
        refs = refs[1:]
    source, own, got, w_qkv, lower_ref, att_low_ref, query_ref, kv_ref, unit_ref, inv_ref = refs[:10]
    lower_low, whole = refs[10:-1], refs[-1]
    if later:
        lower = jnp.where(flags[1] == 1, source[1], before[...].astype(F32))
    else:
        lower = source[0, 1]
    lower = lower - join(own, got, flags[0], whole)
    unit, inv_std = unit_norm(lower)
    att_low = (unit * gains[0:1]).astype(BF16)
    local = query_ref.shape[0]
    kv_ref[...] = dot_t(w_qkv[local:], att_low).astype(BF16)
    query_ref[...] = dot_t(w_qkv[:local], att_low).astype(BF16)
    lower_ref[...] = lower
    att_low_ref[...] = att_low
    unit_ref[...] = unit
    inv_ref[...] = jnp.broadcast_to(inv_std, inv_ref.shape)
    for ref in lower_low:
        ref[...] = lower.astype(BF16)


def attend_kernel(others, flags, *refs):
    query, kv = refs[0], refs[1 : 2 + others]
    w_out, probs_ref, mixed_ref, send, keep, whole = refs[2 + others :]
    local = query.shape[0]
    heads = [slice(at, at + HEAD_DIM) for at in range(0, local, HEAD_DIM)]
    keys = jnp.concatenate([ref[:local, :] for ref in kv], 1)
    values = jnp.concatenate([ref[local:, :] for ref in kv], 1)
    scores = [t_dot(keys[at], query[at, :]) * 0.125 for at in heads]
    weights = [jnp.exp(part - jnp.max(part, 0, keepdims=True)) for part in scores]
    probs = [part * (1.0 / jnp.sum(part, 0, keepdims=True)) for part in weights]
    mixed = [dot(values[at], part.astype(BF16)).astype(BF16) for at, part in zip(heads, probs)]
    for head, at in enumerate(heads):
        probs_ref[head] = probs[head]
        mixed_ref[at, :] = mixed[head]
    whole[...] = t_dot(mixed_ref[...], w_out[...])
    split(whole, flags[0], send, keep)


def attend_back_kernel(later, others, flags, gains, *refs):
    if later:
        before, refs = refs[0], refs[1:]
    source, unit, inv, own, got, query = refs[:6]
    kv = refs[6 : 7 + others]
    refs = refs[7 + others :]
    probs_ref, w_out, total_low_ref, grad_query, kv_own = refs[:5]
    kv_sent = refs[5 : 5 + others]
    totals, whole = refs[5 + others : -1], refs[-1]
    if later:
        total = jnp.where(flags[1] == 1, source[2], before[...].astype(F32))
    else:
        total = source[0, 2]
    grad_normed = join(own, got, flags[0], whole)
    total = total + norm_back(grad_normed, gains[1:2], unit[...], inv[:, 0:1])
    total_low = total.astype(BF16)
    grad_mixed = dot_t(w_out[...], total_low).astype(BF16)
    local, rows = query.shape
    heads = [slice(at, at + HEAD_DIM) for at in range(0, local, HEAD_DIM)]
    keys = jnp.concatenate([ref[:local, :] for ref in kv], 1)
    values = jnp.concatenate([ref[local:, :] for ref in kv], 1)
    probs = [probs_ref[head] for head in range(len(heads))]
    grad_probs = [t_dot(values[at], grad_mixed[at]) for at in heads]
    grad_scores = [
        (p * (g - jnp.sum(p * g, 0, keepdims=True))).astype(BF16) for p, g in zip(probs, grad_probs)
    ]
    grad_values = [dot_t(grad_mixed[at], p.astype(BF16)) for at, p in zip(heads, probs)]
    grad_keys = [0.125 * dot_t(query[at, :], g) for at, g in zip(heads, grad_scores)]
    for head, at in enumerate(heads):
        at_value = slice(local + at.start, local + at.stop)
        kv_own[at, :] = grad_keys[head][:, :rows]
        kv_own[at_value, :] = grad_values[head][:, :rows]
        for number, ref in enumerate(kv_sent):
            cols = slice((number + 1) * rows, (number + 2) * rows)
            ref[at, :] = grad_keys[head][:, cols].astype(BF16)
            ref[at_value, :] = grad_values[head][:, cols].astype(BF16)
        grad_query[at, :] = (0.125 * dot(keys[at], grad_scores[head])).astype(BF16)
    total_low_ref[...] = total_low
    for ref in totals:
        ref[...] = total


def project_back_kernel(others, flags, *refs):
    grad_query, kv_own = refs[:2]
    kv_got = refs[2 : 2 + others]
    mixed, w_qkv, rights, send, keep, whole = refs[2 + others :]
    local = mixed.shape[0]
    total = kv_own[...]
    for ref in kv_got:
        total = total + ref[...].astype(F32)
    rights[:local, :] = grad_query[...]
    rights[local : 3 * local, :] = total.astype(BF16)
    whole[...] = t_dot(rights[: 3 * local, :], w_qkv[...])
    split(whole, flags[0], send, keep)
    rights[3 * local :, :] = mixed[...]


def upper_boundary_kernel(flags, upper, own, got, out):
    total = (own[...].astype(F32) + got[...].astype(F32)).astype(BF16)
    out[...] = (upper[rows_at(flags[0], out.shape[0])] - total.astype(F32)).astype(BF16)


def lower_boundary_kernel(flags, gains, unit, inv, grad_lower, own, got, out):
    rows = rows_at(flags[0], out.shape[0])
    grad_att = (own[...].astype(F32) + got[...].astype(F32)).astype(BF16).astype(F32)
    back = norm_back(grad_att, gains[0:1], unit[rows], inv[rows][:, 0:1])
    out[...] = (grad_lower[rows] + back).astype(BF16)


def recon_middle_kernel(lower_in, total, out, sems):
    copies = start_all(
        [
            pltpu.make_async_copy(lower_in, out.at[0, 1], sems.at[0]),
            pltpu.make_async_copy(total, out.at[0, 2], sems.at[1]),
        ]
    )
    for copy in copies:
        copy.wait()


def recon_upper_kernel(flags, unused, upper, own, got, out, here, sem, whole):
    here[...] = upper[...] - join(own, got, flags[0], whole)
    copy = pltpu.make_async_copy(here, out.at[0, 0], sem)
    copy.start()
    copy.wait()


def recon_lower_kernel(flags, gains, unused, unit, inv, grad_lower, own, got, out, here, sems, whole):
    join(own, got, flags[0], whole)
    copies = []
    for number, rows in enumerate(row_chunks(here.shape[0], 2)):
        back = norm_back(whole[rows], gains[0:1], unit[rows], inv[rows, 0:1])
        here[rows] = grad_lower[rows] + back
        copies.append(pltpu.make_async_copy(here.at[rows], out.at[0, 3, rows], sems.at[number]))
        copies[-1].start()
    for copy in copies:
        copy.wait()


def mlp_grad_kernel(places, *refs):
    out = refs[-1]
    cut, width = out.shape
    left = jnp.concatenate([refs[i][:, at : at + cut] for i, at, unused, unused in places], 0)
    right = jnp.concatenate([refs[i][:, at : at + width] for unused, unused, i, at in places], 0)
    out[...] = t_dot(left, right).astype(BF16)


def att_grad_kernel(count, *refs):
    lefts, rights, qkv, out = refs[:count], refs[count : 2 * count], refs[2 * count], refs[2 * count + 1]
    cut, split_at = out.shape[1], qkv.shape[0]
    right = jnp.concatenate([ref[...] for ref in rights], 1)
    for number, (at, to) in enumerate([(slice(0, split_at), qkv), (slice(split_at, None), out)]):
        left = jnp.concatenate([ref[:, number * cut : (number + 1) * cut] for ref in lefts], 0)
        to[...] = dot(right[at], left).astype(BF16)


def send_message(keep, message, width, count):
    length = lax.axis_size("seq")
    if keep is not None:
        return [keep, shift(message, "seq", 1)]
    place = lax.axis_index("seq")
    cut = width // length

    def at(index):
        lefts = [
            lax.dynamic_slice_in_dim(message[:, i * width : (i + 1) * width], index * cut, cut, 1)
            for i in range(count)
        ]
        return jnp.concatenate(lefts + [message[:, count * width :]], 1)

    return [at(place)] + [
        shift(at((place + by) % length), "seq", by) for by in range(1, length)
    ]


def send_whole(part):
    return [part] + [shift(part, "seq", by) for by in range(1, lax.axis_size("seq"))]


def per_device(streams, head_streams, gains, w_qkv, w_out, w_up, w_down):
    width, local = w_qkv.shape[1], w_qkv.shape[3]
    rows = streams.shape[2]
    n_seq = lax.axis_size("seq")
    others = n_seq - 1
    hidden_width = w_up.shape[2]
    half = rows // 2
    gains = gains[0]
    w_qkv_t = jnp.transpose(w_qkv[0], (1, 2, 0)).reshape(3 * local, width)
    w_out_t = w_out[0].T
    is_last = lax.axis_index("section") == lax.axis_size("section") - 1
    flags = jnp.stack(
        [lax.axis_index("tp") % 2, is_last.astype(jnp.int32), lax.axis_index("seq")]
    ).astype(jnp.int32)
    flag, gain = (flags, "smem"), (gains, "vmem")
    whole, one_sem = pltpu.VMEM((rows, width), F32), pltpu.SemaphoreType.DMA
    full, low = ((rows, width), F32, "vmem"), ((rows, width), BF16, "vmem")
    halves = [((half, width), BF16, "vmem"), ((half, width), F32, "vmem")]
    half_low = halves[0]
    two = n_seq == 2

    left_size = width // 2 if two else width

    def pack(first, second, **more):
        got = run(
            functools.partial(pack_kernel, two),
            [((rows, 2 * left_size), BF16, "vmem")] + [low] * two,
            [flag] + here(first, second),
            **more,
        )
        return (got[1] if two else None), got[0]

    message_outs = [((rows, left_size + hidden_width), BF16, "vmem")]
    keep_outs = [((rows, left_size), BF16, "vmem")] * two
    hid_full = ((rows, hidden_width), F32, "vmem")
    token = None

    def run(body, outs, ins, *rest, **more):
        nonlocal token
        got, token = call(body, outs, ins, *rest, token=token, **more)
        return got

    def here(*arrays):
        return [(a, "vmem") for a in arrays]

    def middle_adds(total):
        by = 2
        while by * 2 < lax.axis_size("tp"):
            (total,) = run(add_kernel, [half_low], here(total, swap(total, "tp", by)))
            by *= 2
        return total, (swap(total, "tp", by) if by < lax.axis_size("tp") else None)

    def add(left, right, **more):
        if right is None:
            return left
        return run(add_kernel, [half_low], here(left, right), **more)[0]

    def zero_if_none(got, like):
        return jnp.zeros_like(like) if got is None else got

    norm_outs = [full, ((rows, 128), F32, "vmem")]
    cut = width // n_seq
    left_width = 2 * cut
    for tick in range(2):
        later = tick > 0
        mlp_outs = message_outs + [hid_full] + halves + norm_outs
        if later:
            got = run(
                mlp_forward_kernel,
                mlp_outs + [full] + keep_outs,
                [flag, gain] + here(got_upper, own_upper, head_streams, up_here, w_down),
                [whole],
            )
            message, slope, send_f, keep_f, unit_up, inv_up, upper = got[:7]
            got_f = swap(send_f, "tp", 1)
            message_2, factors_2 = message, send_message(got[7] if two else None, message, width, 1)
            (next_grad,) = run(
                lower_boundary_kernel,
                [half_low],
                [flag, gain] + here(unit_att, inv_att, grad_lower, sum_b, zero_if_none(got_b, sum_b)),
            )
            own_grad, got_grad = back_to_pair(next_grad)
            sum_f, lower_low, total_low = run(
                add_kernel, [half_low], here(keep_f, got_f), passed=[lower_low, total_low]
            )
            next_lower, next_total = back_a_block(lower_low), back_a_block(total_low)
            sum_f, got_f = middle_adds(sum_f)
            source = here(own_grad, got_grad, head_streams)
        else:
            got = run(
                mlp_first_kernel,
                message_outs
                + [hid_full]
                + norm_outs
                + [full, full, (w_up.shape, BF16, "kept")]
                + keep_outs,
                [flag] + [(a, "hbm") for a in (gains, streams, w_up)],
                [
                    pltpu.VMEM(gains.shape, F32),
                    pltpu.VMEM((rows, width), BF16),
                    pltpu.SemaphoreType.DMA((3 + CHUNKS,)),
                ],
            )
            message, slope, unit_up, inv_up, upper, grad_lower, up_here = got[:7]
            send_f, keep_f = run(mlp_first_down_kernel, halves, [flag] + here(message, w_down), [whole])
            got_f = swap(send_f, "tp", 1)
            message_0, factors_0 = message, send_message(got[7] if two else None, message, width, 1)
            source = here(grad_lower)
        got = run(
            functools.partial(mlp_backward_kernel, later),
            message_outs + halves + [full] * later + keep_outs,
            [flag] + source + here(slope, up_here, w_down),
            [whole],
            after=rights_1[1:] + lefts_1[1:] if later else (),
        )
        message, send_b, keep_b = got[:3]
        keep_left = got[-1] if two else None
        if later:
            grad_lower = got[3]
        got_b = swap(send_b, "tp", 1)
        if later:
            message_3, factors_3 = message, send_message(keep_left, message, width, 1)
            own_out = add(sum_f, got_f, after=())
            got_out = swap(own_out, "tp", 1)
            (sum_b,) = run(add_kernel, [half_low], here(keep_b, got_b))
            sum_b, got_b = middle_adds(sum_b)
        else:
            (sum_f,) = run(add_kernel, [half_low], here(keep_f, got_f))
            sum_f, got_f = middle_adds(sum_f)
            message_1, factors_1 = message, send_message(keep_left, message, width, 1)
            own_out = add(sum_f, got_f)
            got_out = swap(own_out, "tp", 1)
            (sum_b,) = run(add_kernel, [half_low], here(keep_b, got_b), after=())
            sum_b, got_b = middle_adds(sum_b)

        source = here(next_lower, head_streams) if later else here(streams)
        got = run(
            functools.partial(project_kernel, later),
            [full, low, ((local, rows), BF16, "vmem"), ((2 * local, rows), BF16, "vmem")]
            + norm_outs
            + [low] * (not later),
            [flag, gain] + source + here(own_out, got_out, w_qkv_t),
            [whole],
            after=() if later else factors_0[1:],
        )
        lower_in, att_low, query, kv, unit_att, inv_att = got[:6]
        if not later:
            lower_low = got[6]
        all_kv = [kv] + [shift(kv, "seq", -by) for by in range(1, n_seq)]
        own_normed = add(sum_b, got_b, after=factors_2[1:] if later else ())
        got_normed = swap(own_normed, "tp", 1)
        probs, mixed, send_f, keep_f = run(
            functools.partial(attend_kernel, others),
            [((local // HEAD_DIM, n_seq * rows, rows), F32, "vmem"), ((local, rows), BF16, "vmem")]
            + halves,
            [flag] + here(query, *all_kv, w_out_t),
            [whole],
            after=() if later else factors_1[1:],
        )
        got_f = swap(send_f, "tp", 1)

        got = run(
            functools.partial(attend_back_kernel, later, others),
            [low, ((local, rows), BF16, "vmem"), ((2 * local, rows), F32, "vmem")]
            + [((2 * local, rows), BF16, "vmem")] * others
            + [full] * later,
            [flag, gain]
            + (here(next_total, head_streams) if later else here(streams))
            + here(unit_up, inv_up, own_normed, got_normed, query, *all_kv, probs, w_out_t),
            [whole],
            after=factors_3[1:] if later else (),
        )
        total_low, grad_query, kv_own = got[:3]
        kv_got = [shift(part, "seq", by + 1) for by, part in enumerate(got[3 : 3 + others])]
        if not later:
            (sum_f,) = run(add_kernel, [half_low], here(keep_f, got_f))
            sum_f, got_f = middle_adds(sum_f)
        else:
            recon_out = [((1, 4, rows, width), F32, "any")]
            (recon,) = run(
                recon_middle_kernel, recon_out, here(lower_in, got[-1]), [pltpu.SemaphoreType.DMA((2,))]
            )
        rights, send_b, keep_b = run(
            functools.partial(project_back_kernel, others),
            [((4 * local, rows), BF16, "vmem")] + halves,
            [flag] + here(grad_query, kv_own, *kv_got, mixed, w_qkv_t),
            [whole],
            after=() if later else (),
        )
        got_b = swap(send_b, "tp", 1)
        rights_att = send_whole(rights)

        if later:
            rights_2 = rights_att
            (sum_f,) = run(add_kernel, [half_low], here(keep_f, got_f))
            sum_f, got_f = middle_adds(sum_f)
            lefts_2 = send_message(*pack(att_low, total_low), width, 2)
            (sum_b,) = run(add_kernel, [half_low], here(keep_b, got_b))
            sum_b, got_b = middle_adds(sum_b)
            own_f = add(sum_f, got_f)
            got_f = swap(own_f, "tp", 1)
        else:
            rights_1 = rights_att
            (next_half,) = run(
                upper_boundary_kernel,
                [half_low],
                [flag] + here(upper, sum_f, zero_if_none(got_f, sum_f)),
            )
            (sum_b,) = run(add_kernel, [half_low], here(keep_b, got_b))
            sum_b, got_b = middle_adds(sum_b)
            own_upper, got_upper = back_to_pair(next_half)
            lefts_1 = send_message(*pack(att_low, total_low), width, 2)

    ups, downs = [], []
    for up, down, mine_up, mine_down in (
        (factors_0, factors_1, message_1, message_0),
        (factors_2, factors_3, message_3, message_2),
    ):
        ups.append((up[0], 0, mine_up, left_size))
        downs.append((down[0], 0, mine_down, left_size))
        for i in range(1, n_seq):
            ups.append((up[i], 0, down[i], cut))
            downs.append((down[i], 0, up[i], cut))

    def mlp_grad(terms):
        if not two:
            left = jnp.concatenate([a[:, at : at + cut] for a, at, unused, unused in terms], 0)
            right = jnp.concatenate([a[:, at : at + hidden_width] for unused, unused, a, at in terms], 0)
            return t_dot(left, right).astype(BF16)
        arrays, places = [], []
        for left, left_at, right, right_at in terms:
            for array in (left, right):
                if not any(array is known for known in arrays):
                    arrays.append(array)
            where = [next(i for i, known in enumerate(arrays) if known is a) for a in (left, right)]
            places.append((where[0], left_at, where[1], right_at))
        (grad,) = run(
            functools.partial(mlp_grad_kernel, places),
            [((cut, hidden_width), BF16, "vmem")],
            here(*arrays),
        )
        return grad

    grad_down = mlp_grad(downs)
    grad_up = mlp_grad(ups)
    own_b = add(sum_b, got_b)
    got_b = swap(own_b, "tp", 1)
    (recon,) = run(
        recon_upper_kernel,
        recon_out,
        [flag, (recon, "any")] + here(upper, own_f, got_f),
        [whole, one_sem, whole],
        aliases=[(1, 0)],
    )
    lefts_att, rights_att = lefts_1 + lefts_2, rights_1 + rights_2
    if two:
        grad_qkv, grad_out = run(
            functools.partial(att_grad_kernel, len(rights_att)),
            [((3 * local, cut), BF16, "vmem"), ((local, cut), BF16, "vmem")],
            here(*lefts_att, *rights_att),
        )
    else:
        right = jnp.concatenate(rights_att, 1)
        left = jnp.concatenate([a[:, :left_width] for a in lefts_att], 0)
        grad_qkv = dot(right[: 3 * local], left[:, :cut]).astype(BF16)
        grad_out = dot(right[3 * local :], left[:, cut:]).astype(BF16)
    (recon,) = run(
        recon_lower_kernel,
        recon_out,
        [flag, gain, (recon, "any")] + here(unit_att, inv_att, grad_lower, own_b, got_b),
        [whole, pltpu.SemaphoreType.DMA((2,)), whole],
        aliases=[(2, 0)],
    )
    return (
        recon,
        jnp.transpose(grad_qkv.reshape(3, local, cut), (2, 0, 1))[None],
        grad_out.T[None],
        grad_up[None],
        grad_down[None],
    )


def solution(mesh):
    placed = (
        P("section", None, "seq", None),
        P(None, "seq", None),
        P("section", None, None),
        P("section", None, None, "tp"),
        P("section", None, "tp"),
        P("section", None, "tp"),
        P("section", None, "tp"),
    )
    return jax.shard_map(
        per_device,
        mesh=mesh,
        in_specs=placed,
        out_specs=(
            P("section", None, "seq", None),
            P("section", "seq", None, "tp"),
            P("section", "seq", "tp"),
            P("section", "seq", "tp"),
            P("section", "seq", "tp"),
        ),
        check_vma=False,
    )
```
